256 devices in a mesh: sec: 4 (over y), gx: 64 (over x, z, core).
Axes of the slice: x: 4, y: 4, z: 8, core: 2. Of those that a mesh axis runs over, the one named last changes fastest.
Arguments:
- pressure_start: float32 [16, 1024, 1024], P('sec', 'gx'), may hold values from -8 to 8
- soil_type: int32 [16, 1024, 1024], P('sec', 'gx'), may hold values from 0 to 11
- saturated_conductivity: float32 [12], replicated, may hold values from 0.2 to 5
- storage_coefficient: float32 [12], replicated, may hold values from 0.1 to 1
- rainfall: float32 [3, 1024, 1024], P(None, 'gx'), may hold values from 0 to 2
Outputs:
- pressure: float32 [16, 1024, 1024], P('sec', 'gx')
- inflow: float32 [4, 3, 1024, 1024], P('sec', None, 'gx')
The draws below stay inside these ranges and needn't reach their ends.
All inputs are finite; a program needn't handle non-finite values.
Results may differ from the reference program's by a relative error of at most 0.0001.
Values sent between devices are 32-bit elements; how exact they have to be, the bound alone decides.
No kernel may reach another device: no remote copies, remote signals or barrier semaphores. Data moves between devices by JAX's collectives and lax.ppermute only.
A program may use at most 64 MiB of HBM per device.

```python
import math
import jax
import jax.numpy as jnp

LZ = 4
STEPS = 3
ITERS = 4
SOILS = 12
NZ = 16
NX = 1024
NY = 1024
N_SEC = 4


def touch_ends(array, stream_key, low, high):
    longest = array.shape.index(max(array.shape))
    spots = []
    for shift in (0, 1):
        where = [jax.random.randint(jax.random.fold_in(stream_key, axis), (), 0, length) for axis, length in enumerate(array.shape)]
        where[longest] = (where[longest] + shift) % array.shape[longest]
        spots.append(tuple(where))
    return array.at[spots[0]].set(low).at[spots[1]].set(high)


def levels(rng, extent, split, smallest, largest):
    factor_of = 1.0
    for axis_at, parts in split:
        steps = jax.random.uniform(jax.random.fold_in(jax.random.fold_in(rng, 6), axis_at), (parts,), jnp.float32, smallest / len(split), largest / len(split))
        factor_of = factor_of * jnp.repeat(jnp.exp(steps), extent[axis_at] // parts).reshape((-1,) + (1,) * (len(extent) - 1 - axis_at))
    return factor_of


def bell_draw(stream_key, dims, deviation, bound, split=(), held_as=jnp.bfloat16):
    values = jax.random.normal(stream_key, dims, jnp.float32) * deviation
    if len(split) > 0:
        values = levels(stream_key, dims, split, -0.22, 0.18) * values
    return jnp.clip(values, min=-bound, max=bound).astype(held_as)


def setup_inputs(seed: int = 0) -> dict:
    key_list = jax.random.split(jax.random.key(seed), 6)
    return {
        "pressure_start": bell_draw(key_list[0], (NZ, NX, NY), 1.5, 8.0, ((0, 4), (1, 64)), jnp.float32),
        "soil_type": touch_ends(jax.random.randint(key_list[1], (NZ, NX, NY), 0, SOILS), jax.random.fold_in(key_list[1], 1), 0, SOILS - 1).astype(jnp.int32),
        "saturated_conductivity": jnp.clip(jnp.exp(jax.random.uniform(key_list[2], (SOILS,), jnp.float32, math.log(0.2), math.log(5.0))), 0.2, 5.0),
        "storage_coefficient": jnp.clip(jnp.exp(jax.random.uniform(key_list[3], (SOILS,), jnp.float32, math.log(0.1), math.log(1.0))), 0.1, 1.0),
        "rainfall": jnp.clip(2.0 * jax.random.uniform(key_list[4], (STEPS, NX, NY), jnp.float32) ** levels(key_list[4], (STEPS, NX, NY), ((1, 64),), -0.2, 0.2), 0.0, 2.0),
    }


def harmonic(cond, other):
    return 2.0 * cond * other / (cond + other)


def neighbours(padded):
    return [padded[:-2, 1:-1, 1:-1], padded[2:, 1:-1, 1:-1], padded[1:-1, :-2, 1:-1],
            padded[1:-1, 2:, 1:-1], padded[1:-1, 1:-1, :-2], padded[1:-1, 1:-1, 2:]]


def operate(field, faces, capacity):
    result = capacity * field
    for face, other in zip(faces, neighbours(jnp.pad(field, 1))):
        result = result + face * (field - other)
    return result


def reference(pressure_start, soil_type, saturated_conductivity, storage_coefficient, rainfall):
    cond_table = saturated_conductivity[soil_type]
    store_table = storage_coefficient[soil_type]
    head = pressure_start
    flows = []
    for step in range(STEPS):
        saturation = jax.nn.sigmoid(head)
        conductivity = cond_table * (0.05 + saturation * saturation)
        capacity = store_table * (0.1 + saturation * (1.0 - saturation))
        faces = [harmonic(conductivity, other) for other in neighbours(jnp.pad(conductivity, 1))]
        water = jnp.sum(saturation.reshape(N_SEC, LZ, NX, NY), axis=1)
        bottom = conductivity.reshape(N_SEC, LZ, NX, NY)[:, LZ - 1]
        depth = jnp.float32(LZ)
        below = jnp.zeros((NX, NY), jnp.float32)
        slopes = [None] * N_SEC
        for section in reversed(range(N_SEC)):
            slopes[section] = (water[section] / depth) * (0.5 + 0.5 * below / (below + depth))
            below = below + water[section]
        prefix_a = jnp.ones((NX, NY), jnp.float32)
        prefix_b = jnp.zeros((NX, NY), jnp.float32)
        inflows = []
        sources = []
        for section in range(N_SEC):
            entering = prefix_a * rainfall[step] + prefix_b
            offset = 0.5 * bottom[section]
            leaving = slopes[section] * entering + offset
            inflows.append(entering)
            local = jnp.zeros((LZ, NX, NY), jnp.float32).at[0].add(entering).at[LZ - 1].add(-leaving)
            sources.append(local)
            prefix_b = slopes[section] * prefix_b + offset
            prefix_a = slopes[section] * prefix_a
        flows.append(jnp.stack(inflows))
        source = jnp.concatenate(sources, axis=0)
        gravity = faces[0] - faces[1]
        rhs = capacity * head + gravity + source
        diagonal = capacity
        for face in faces:
            diagonal = diagonal + face
        iterate = head
        residual = rhs - operate(iterate, faces, capacity)
        precond = residual / diagonal
        direction = precond
        product = jnp.sum(residual * precond)
        for turn in range(ITERS):
            image = operate(direction, faces, capacity)
            alpha = product / jnp.sum(direction * image)
            iterate = iterate + alpha * direction
            residual = residual - alpha * image
            if turn + 1 < ITERS:
                precond = residual / diagonal
                renewed = jnp.sum(residual * precond)
                direction = precond + (renewed / product) * direction
                product = renewed
        head = iterate
    return head, jnp.stack(flows, axis=1)
```

```python
import functools

import jax
import jax.numpy as jnp
from jax import lax
from jax.experimental import pallas as pl
from jax.experimental.pallas import tpu as pltpu
from jax.sharding import PartitionSpec as P

ITERS = 4
SECTIONS = 4
LZ = 4
NZ = SECTIONS * LZ
OWN_ROWS = 16
OWN_COLS = 256
WIDE = 384
HALF = 64
FRAME = 48
SPANS = ((0, 48), (0, 40), (8, 40))
F32 = jnp.float32
VMEM = pl.BlockSpec(memory_space=pltpu.VMEM)


def params():
    return pltpu.CompilerParams(vmem_limit_bytes=56 * 1024 * 1024)


def pack_kernel(head_ref, soil_ref, rain_ref, out_ref):
    section = lax.axis_index("sec")
    low_half = lax.broadcasted_iota(jnp.int32, (OWN_ROWS, 128), 1) < HALF
    rain_step = jnp.minimum(section, 2)
    for target in range(SECTIONS):
        start = target * OWN_COLS
        after = (start + OWN_COLS) % (SECTIONS * OWN_COLS)
        before = (start - 128) % (SECTIONS * OWN_COLS)

        def put(slot, read):
            out_ref[target, slot, :, 0:OWN_COLS] = read(start, OWN_COLS)
            out_ref[target, slot, :, OWN_COLS:WIDE] = jnp.where(low_half, read(after, 128), read(before, 128))

        for q in range(LZ):
            put(q, lambda at, n: head_ref[q, :, at : at + n])
            put(LZ + q, lambda at, n: soil_ref[q, :, at : at + n].astype(F32))
        put(2 * LZ, lambda at, n: rain_ref[rain_step, :, at : at + n])


def weights(sums_ref):
    total = jnp.sum(sums_ref[...], axis=0, keepdims=True)
    lane = lax.broadcasted_iota(jnp.int32, total.shape, 1)
    m = [jnp.sum(jnp.where(lane == k, total, 0.0), axis=1, keepdims=True) for k in range(8)]
    step_m = [m[k] - m[k + 1] for k in range(7)]
    zero = jnp.zeros_like(m[0])

    def form(poly, other, table):
        result = zero
        for i, a in enumerate(poly):
            for j, b in enumerate(other):
                result = result + a * b * table[i + j]
        return result

    z = [jnp.ones_like(zero)]
    direction = z
    rz = m[0]
    change = [zero] * ITERS
    for turn in range(ITERS):
        below = form(direction, direction, step_m)
        alpha = jnp.where(below > 0.0, rz / jnp.where(below > 0.0, below, 1.0), 0.0)
        for i, a in enumerate(direction):
            change[i] = change[i] + alpha * a
        if turn + 1 < ITERS:
            long = direction + [zero]
            image = [long[i] - (long[i - 1] if i else zero) for i in range(len(long))]
            z = [a - alpha * b for a, b in zip(z + [zero], image)]
            renewed = form(z, z, m)
            beta = jnp.where(rz > 0.0, renewed / jnp.where(rz > 0.0, rz, 1.0), 0.0)
            direction = [a + beta * b for a, b in zip(z, long)]
            rz = renewed
    return change


def recip(x):
    return pl.reciprocal(x, approx=False)


def setup_terms(h, cond_table, store_table):
    saturation = recip(1.0 + jnp.exp(-h))
    cond = cond_table * (0.05 + saturation * saturation)
    capacity = store_table * (0.1 + saturation * (1.0 - saturation))
    return saturation, cond, capacity


def gather(table, kinds):
    rows, cols = kinds.shape
    parts = []
    for j in range(cols // 128):
        parts.append(
            jnp.concatenate(
                [
                    jnp.take_along_axis(table, kinds[8 * i : 8 * i + 8, 128 * j : 128 * j + 128], axis=1, mode="promise_in_bounds")
                    for i in range(rows // 8)
                ],
                axis=0,
            )
        )
    return jnp.concatenate(parts, axis=1)


def step_kernel(step, n_rows_all, *refs):
    first = step == 0
    r0, r1 = SPANS[step]
    rows = r1 - r0
    own = OWN_ROWS - r0
    if first:
        (low_ref, mid_ref, high_ref, tables_ref, head_ref, cond_ref, store_ref, rain_ref) = refs[:8]
        refs = refs[8:]
    else:
        p0 = SPANS[step - 1][0]
        old = slice(r0 - p0, r1 - p0)
        (sums_ref, old_head_ref, o0, o1, o2, o3, cond_ref, store_ref, rain_ref, head_ref) = refs[:10]
        old_basis = (o0, o1, o2, o3)
        refs = refs[10:]
    (v0, v1, v2, v3, inflow_ref, moments_ref) = refs[:6]
    (res_ref, cap_ref, diag_ref, face_ref, up_ref, dn_ref, ru_ref, rd_ref, xl_ref, xr_ref, water_ref, low_cond_ref, flux_ref) = refs[6:]
    basis = (v0, v1, v2, v3)
    here = slice(r0, r1)
    section, band = lax.axis_index("sec"), lax.axis_index("gx")

    if first:
        for s in range(3):
            rain_ref[s, 0:16, :] = low_ref[s, 8]
            rain_ref[s, 16:32, :] = mid_ref[s, 8]
            rain_ref[s, 32:48, :] = high_ref[s, 8]
    else:
        change = weights(sums_ref)

    def soil(s, carry):
        total = jnp.zeros((rows, WIDE), F32)
        for q in range(LZ):
            l = s * LZ + q
            if first:
                for part, ref in enumerate((low_ref, mid_ref, high_ref)):
                    at = slice(16 * part, 16 * part + 16)
                    kinds = ref[s, LZ + q].astype(jnp.int32)
                    head_ref[l, at, :] = ref[s, q]
                    cond_ref[l, at, :] = gather(tables_ref[0], kinds)
                    store_ref[l, at, :] = gather(tables_ref[1], kinds)
                h = head_ref[l]
            else:
                h = old_head_ref[l, old, :]
                for c, o in zip(change, old_basis):
                    h = h + c * o[l, old, :]
                head_ref[l] = h
            saturation, cond, capacity = setup_terms(h, cond_ref[l, here, :], store_ref[l, here, :])
            res_ref[l] = recip(cond)
            cap_ref[l] = capacity
            total = total + saturation
            if q == LZ - 1:
                low_cond_ref[s] = 0.5 * cond
        water_ref[s] = total
        return carry

    lax.fori_loop(0, SECTIONS, soil, 0)

    flux_ref[0] = rain_ref[step, here, :]
    belows = [None] * SECTIONS
    below = None
    for s in reversed(range(SECTIONS)):
        belows[s] = below
        below = water_ref[s] if below is None else below + water_ref[s]
    for s in range(SECTIONS):
        scale = 0.5 if belows[s] is None else 0.5 + 0.5 * belows[s] / (belows[s] + 4.0)
        flux_ref[s + 1] = water_ref[s] * 0.25 * scale * flux_ref[s] + low_cond_ref[s]
        inflow_ref[s] = flux_ref[s, own : own + OWN_ROWS, 0:OWN_COLS]

    lane = lax.broadcasted_iota(jnp.int32, (rows, WIDE), 1)
    col = section * OWN_COLS + lane - jnp.where(lane >= OWN_COLS + HALF, WIDE, 0)
    row = band * OWN_ROWS + (r0 - OWN_ROWS) + lax.broadcasted_iota(jnp.int32, (rows, WIDE), 0)
    col_gate = jnp.where((col >= 1) & (col < SECTIONS * OWN_COLS), 2.0, 0.0).astype(F32)
    row_gate = jnp.where((row >= 1) & (row < n_rows_all), 2.0, 0.0).astype(F32)
    kept = slice(own, own + OWN_ROWS)
    none = jnp.zeros((OWN_ROWS, OWN_COLS), F32)

    face_ref[0] = jnp.zeros((rows, WIDE), F32)

    def faces(s, acc):
        for q in range(LZ):
            l = s * LZ + q
            res = res_ref[l]
            up = face_ref[l]
            after = jnp.minimum(l + 1, NZ - 1)
            dn = jnp.where(l < NZ - 1, 2.0, 0.0).astype(F32) * recip(res + res_ref[after])
            face_ref[l + 1] = dn
            ru = row_gate * recip(res + pltpu.roll(res, 1, 0))
            rd = pltpu.roll(ru, rows - 1, 0)
            xl = col_gate * recip(res + pltpu.roll(res, 1, 1))
            xr = pltpu.roll(xl, WIDE - 1, 1)
            diag = cap_ref[l] + up + dn + ru + rd + xl + xr
            inv = recip(diag)
            h = head_ref[l]
            r = up - dn
            if q == 0:
                r = r + flux_ref[s]
            if q == LZ - 1:
                r = r - flux_ref[s + 1]
            r = r + up * (head_ref[jnp.maximum(l - 1, 0)] - h) + dn * (head_ref[after] - h)
            r = r + ru * (pltpu.roll(h, 1, 0) - h) + rd * (pltpu.roll(h, rows - 1, 0) - h)
            r = r + xl * (pltpu.roll(h, 1, 1) - h) + xr * (pltpu.roll(h, WIDE - 1, 1) - h)
            z = r * inv
            v0[l] = z
            diag_ref[l] = diag
            up_ref[l] = up * inv
            dn_ref[l] = dn * inv
            ru_ref[l] = ru * inv
            rd_ref[l] = rd * inv
            xl_ref[l] = xl * inv
            xr_ref[l] = xr * inv
            acc = acc + (r * z)[kept, 0:OWN_COLS]
        return acc

    moments = [lax.fori_loop(0, SECTIONS, faces, none)]

    for k in range(1, ITERS):
        src, dst = basis[k - 1], basis[k]

        def smooth(l, accs, src=src, dst=dst):
            v = src[l]
            new = up_ref[l] * src[jnp.maximum(l - 1, 0)] + dn_ref[l] * src[jnp.minimum(l + 1, NZ - 1)]
            new = new + ru_ref[l] * pltpu.roll(v, 1, 0) + rd_ref[l] * pltpu.roll(v, rows - 1, 0)
            new = new + xl_ref[l] * pltpu.roll(v, 1, 1) + xr_ref[l] * pltpu.roll(v, WIDE - 1, 1)
            dst[l] = new
            mine = new[kept, 0:OWN_COLS]
            scaled = mine * diag_ref[l, kept, 0:OWN_COLS]
            return accs[0] + v[kept, 0:OWN_COLS] * scaled, accs[1] + mine * scaled

        moments.extend(lax.fori_loop(0, NZ, smooth, (none, none)))

    def last(l, acc):
        block = slice(own - 8, own + OWN_ROWS)
        v = v3[l, block, :]
        mine = v[8:, 0:OWN_COLS]
        pairs = up_ref[l, kept, 0:OWN_COLS] * v3[jnp.maximum(l - 1, 0), kept, 0:OWN_COLS]
        pairs = pairs + ru_ref[l, kept, 0:OWN_COLS] * pltpu.roll(v, 1, 0)[8:, 0:OWN_COLS]
        pairs = pairs + xl_ref[l, kept, 0:OWN_COLS] * pltpu.roll(v, 1, 1)[8:, 0:OWN_COLS]
        return acc + 2.0 * mine * diag_ref[l, kept, 0:OWN_COLS] * pairs

    moments.append(lax.fori_loop(0, NZ, last, none))

    spot = lax.broadcasted_iota(jnp.int32, (8, 128), 1)
    line = jnp.zeros((8, 128), F32)
    for k, acc in enumerate(moments):
        value = jnp.sum(jnp.sum(acc, axis=0, keepdims=True), axis=1, keepdims=True)
        line = jnp.where(spot == k, value, line)
    for i in range(moments_ref.shape[0] // 8):
        moments_ref[8 * i : 8 * i + 8, :] = line


def last_kernel(sums_ref, head_ref, v0, v1, v2, v3, i0, i1, i2, out_ref):
    change = weights(sums_ref)
    own = OWN_ROWS - SPANS[2][0]
    kept = slice(own, own + OWN_ROWS)
    for l in range(NZ):
        h = head_ref[l, kept, 0:OWN_COLS]
        for c, o in zip(change, (v0, v1, v2, v3)):
            h = h + c * o[l, kept, 0:OWN_COLS]
        out_ref[l // LZ, l % LZ] = h
    for s in range(SECTIONS):
        for c, i in enumerate((i0, i1, i2)):
            out_ref[s, LZ + c] = i[s]


def shape(*dims):
    return jax.ShapeDtypeStruct(dims, F32)


def call(kernel, operands, outs, scratch=()):
    return pl.pallas_call(
        kernel,
        out_shape=outs,
        in_specs=[VMEM] * len(operands),
        out_specs=jax.tree.map(lambda _: VMEM, outs),
        scratch_shapes=[pltpu.VMEM(dims, F32) for dims in scratch],
        compiler_params=params(),
    )(*operands)


def add_up(moments):
    return lax.all_to_all(moments, ("sec", "gx"), 0, 0, tiled=True)


def body(pressure_start, soil_type, saturated_conductivity, storage_coefficient, rainfall):
    bands = lax.axis_size("gx")
    devices = SECTIONS * bands
    packed = call(pack_kernel, (pressure_start, soil_type, rainfall), shape(SECTIONS, 9, OWN_ROWS, WIDE))
    mid = lax.all_to_all(packed, "sec", 0, 0, tiled=True)
    low = lax.ppermute(mid, "gx", [(i, i + 1) for i in range(bands - 1)])
    high = lax.ppermute(mid, "gx", [(i + 1, i) for i in range(bands - 1)])
    tables = jnp.stack([saturated_conductivity, storage_coefficient])
    tables = jnp.broadcast_to(jnp.pad(tables, ((0, 0), (0, 128 - tables.shape[1])))[:, None, :], (2, 8, 128))
    inflows = []
    state = None
    for step, (r0, r1) in enumerate(SPANS):
        rows = r1 - r0
        field = (NZ, rows, WIDE)
        wide = (NZ, FRAME, WIDE)
        outs = [shape(*field)] * 5
        kernel = functools.partial(step_kernel, step, bands * OWN_ROWS)
        tail = [shape(SECTIONS, OWN_ROWS, OWN_COLS), shape(devices, 128)]
        scratch = [field, field, field, (NZ + 1, rows, WIDE)] + [field] * 6 + [(SECTIONS, rows, WIDE)] * 2 + [(SECTIONS + 1, rows, WIDE)]
        if step == 0:
            outs = [shape(*field), shape(*wide), shape(*wide), shape(3, FRAME, WIDE)] + [shape(*field)] * 4
            got = call(kernel, (low, mid, high, tables), outs + tail, scratch)
            head, cond, store, rain = got[:4]
            v = got[4:8]
        else:
            got = call(kernel, (sums, head, *v, cond, store, rain), outs + tail, scratch)
            head, v = got[0], got[1:5]
        inflows.append(got[-2])
        sums = add_up(got[-1])
    out = call(last_kernel, (sums, head, *v, *inflows), shape(SECTIONS, 7, OWN_ROWS, OWN_COLS))
    out = lax.all_to_all(out, "sec", 0, 0, tiled=True)
    out = jnp.transpose(out, (1, 2, 0, 3)).reshape(7, OWN_ROWS, SECTIONS * OWN_COLS)
    return out[:LZ], out[LZ:][None]


def solution(mesh):
    placed = (P("sec", "gx", None), P("sec", "gx", None), P(), P(), P(None, "gx", None))
    return jax.shard_map(
        body,
        mesh=mesh,
        in_specs=placed,
        out_specs=(P("sec", "gx", None), P("sec", None, "gx", None)),
        check_vma=False,
    )
```

```python
import functools

import jax
import jax.numpy as jnp
from jax import lax
from jax.experimental import pallas as pl
from jax.experimental.pallas import tpu as pltpu
from jax.sharding import PartitionSpec as P

ITERS = 4
SECTIONS = 4
LZ = 4
NZ = SECTIONS * LZ
OWN_ROWS = 16
OWN_COLS = 256
WIDE = 384
HALF = 64
FRAME = 48
SPANS = ((0, 48), (0, 40), (8, 40))
F32 = jnp.float32
VMEM = pl.BlockSpec(memory_space=pltpu.VMEM)


def params():
    return pltpu.CompilerParams(vmem_limit_bytes=24 * 1024 * 1024)


def pack_kernel(head_ref, soil_ref, rain_ref, out_ref):
    section = lax.axis_index("sec")
    low_half = lax.broadcasted_iota(jnp.int32, (OWN_ROWS, 128), 1) < HALF
    rain_step = jnp.minimum(section, 2)
    for target in range(SECTIONS):
        start = target * OWN_COLS
        after = (start + OWN_COLS) % (SECTIONS * OWN_COLS)
        before = (start - 128) % (SECTIONS * OWN_COLS)

        def put(slot, read):
            out_ref[target, slot, :, 0:OWN_COLS] = read(start, OWN_COLS)
            out_ref[target, slot, :, OWN_COLS:WIDE] = jnp.where(low_half, read(after, 128), read(before, 128))

        for q in range(LZ):
            put(q, lambda at, n: head_ref[q, :, at : at + n])
            put(LZ + q, lambda at, n: soil_ref[q, :, at : at + n].astype(F32))
        put(2 * LZ, lambda at, n: rain_ref[rain_step, :, at : at + n])


def weights(sums_ref):
    total = jnp.sum(sums_ref[...], axis=0, keepdims=True)
    lane = lax.broadcasted_iota(jnp.int32, total.shape, 1)
    m = [jnp.sum(jnp.where(lane == k, total, 0.0), axis=1, keepdims=True) for k in range(8)]
    step_m = [m[k] - m[k + 1] for k in range(7)]
    zero = jnp.zeros_like(m[0])

    def form(poly, other, table):
        result = zero
        for i, a in enumerate(poly):
            for j, b in enumerate(other):
                result = result + a * b * table[i + j]
        return result

    z = [jnp.ones_like(zero)]
    direction = z
    rz = m[0]
    change = [zero] * ITERS
    for turn in range(ITERS):
        below = form(direction, direction, step_m)
        alpha = jnp.where(below > 0.0, rz / jnp.where(below > 0.0, below, 1.0), 0.0)
        for i, a in enumerate(direction):
            change[i] = change[i] + alpha * a
        if turn + 1 < ITERS:
            long = direction + [zero]
            image = [long[i] - (long[i - 1] if i else zero) for i in range(len(long))]
            z = [a - alpha * b for a, b in zip(z + [zero], image)]
            renewed = form(z, z, m)
            beta = jnp.where(rz > 0.0, renewed / jnp.where(rz > 0.0, rz, 1.0), 0.0)
            direction = [a + beta * b for a, b in zip(z, long)]
            rz = renewed
    return change


def recip(x):
    return pl.reciprocal(x, approx=False)


def setup_terms(h, cond_table, store_table):
    saturation = recip(1.0 + jnp.exp(-h))
    cond = cond_table * (0.05 + saturation * saturation)
    capacity = store_table * (0.1 + saturation * (1.0 - saturation))
    return saturation, cond, capacity


def gather(table, kinds):
    rows, cols = kinds.shape
    parts = []
    for j in range(cols // 128):
        parts.append(
            jnp.concatenate(
                [
                    jnp.take_along_axis(table, kinds[8 * i : 8 * i + 8, 128 * j : 128 * j + 128], axis=1, mode="promise_in_bounds")
                    for i in range(rows // 8)
                ],
                axis=0,
            )
        )
    return jnp.concatenate(parts, axis=1)


def step_kernel(step, n_rows_all, *refs):
    first = step == 0
    r0, r1 = SPANS[step]
    rows = r1 - r0
    own = OWN_ROWS - r0
    if first:
        (low_ref, mid_ref, high_ref, tables_ref, head_ref, cond_ref, store_ref, rain_ref) = refs[:8]
        refs = refs[8:]
    else:
        p0 = SPANS[step - 1][0]
        old = slice(r0 - p0, r1 - p0)
        (sums_ref, old_head_ref, o0, o1, o2, o3, cond_ref, store_ref, rain_ref, head_ref) = refs[:10]
        old_basis = (o0, o1, o2, o3)
        refs = refs[10:]
    (v0, v1, v2, v3, inflow_ref, moments_ref) = refs[:6]
    (res_ref, cap_ref, diag_ref, face_ref, up_ref, dn_ref, ru_ref, rd_ref, xl_ref, xr_ref, water_ref, low_cond_ref, flux_ref) = refs[6:]
    basis = (v0, v1, v2, v3)
    here = slice(r0, r1)
    section, band = lax.axis_index("sec"), lax.axis_index("gx")

    if first:
        for s in range(3):
            rain_ref[s, 0:16, :] = low_ref[s, 8]
            rain_ref[s, 16:32, :] = mid_ref[s, 8]
            rain_ref[s, 32:48, :] = high_ref[s, 8]
    else:
        change = weights(sums_ref)

    def soil(s, carry):
        total = jnp.zeros((rows, WIDE), F32)
        for q in range(LZ):
            l = s * LZ + q
            if first:
                for part, ref in enumerate((low_ref, mid_ref, high_ref)):
                    at = slice(16 * part, 16 * part + 16)
                    kinds = ref[s, LZ + q].astype(jnp.int32)
                    head_ref[l, at, :] = ref[s, q]
                    cond_ref[l, at, :] = gather(tables_ref[0], kinds)
                    store_ref[l, at, :] = gather(tables_ref[1], kinds)
                h = head_ref[l]
            else:
                h = old_head_ref[l, old, :]
                for c, o in zip(change, old_basis):
                    h = h + c * o[l, old, :]
                head_ref[l] = h
            saturation, cond, capacity = setup_terms(h, cond_ref[l, here, :], store_ref[l, here, :])
            res_ref[l] = recip(cond)
            cap_ref[l] = capacity
            total = total + saturation
            if q == LZ - 1:
                low_cond_ref[s] = 0.5 * cond
        water_ref[s] = total
        return carry

    lax.fori_loop(0, SECTIONS, soil, 0)

    flux_ref[0] = rain_ref[step, here, :]
    belows = [None] * SECTIONS
    below = None
    for s in reversed(range(SECTIONS)):
        belows[s] = below
        below = water_ref[s] if below is None else below + water_ref[s]
    for s in range(SECTIONS):
        scale = 0.5 if belows[s] is None else 0.5 + 0.5 * belows[s] / (belows[s] + 4.0)
        flux_ref[s + 1] = water_ref[s] * 0.25 * scale * flux_ref[s] + low_cond_ref[s]
        inflow_ref[s] = flux_ref[s, own : own + OWN_ROWS, 0:OWN_COLS]

    lane = lax.broadcasted_iota(jnp.int32, (rows, WIDE), 1)
    col = section * OWN_COLS + lane - jnp.where(lane >= OWN_COLS + HALF, WIDE, 0)
    row = band * OWN_ROWS + (r0 - OWN_ROWS) + lax.broadcasted_iota(jnp.int32, (rows, WIDE), 0)
    col_gate = jnp.where((col >= 1) & (col < SECTIONS * OWN_COLS), 2.0, 0.0).astype(F32)
    row_gate = jnp.where((row >= 1) & (row < n_rows_all), 2.0, 0.0).astype(F32)
    kept = slice(own, own + OWN_ROWS)
    none = jnp.zeros((OWN_ROWS, OWN_COLS), F32)

    face_ref[0] = jnp.zeros((rows, WIDE), F32)

    def faces(s, acc):
        for q in range(LZ):
            l = s * LZ + q
            res = res_ref[l]
            up = face_ref[l]
            after = jnp.minimum(l + 1, NZ - 1)
            dn = jnp.where(l < NZ - 1, 2.0, 0.0).astype(F32) * recip(res + res_ref[after])
            face_ref[l + 1] = dn
            ru = row_gate * recip(res + pltpu.roll(res, 1, 0))
            rd = pltpu.roll(ru, rows - 1, 0)
            xl = col_gate * recip(res + pltpu.roll(res, 1, 1))
            xr = pltpu.roll(xl, WIDE - 1, 1)
            diag = cap_ref[l] + up + dn + ru + rd + xl + xr
            inv = recip(diag)
            h = head_ref[l]
            r = up - dn
            if q == 0:
                r = r + flux_ref[s]
            if q == LZ - 1:
                r = r - flux_ref[s + 1]
            r = r + up * (head_ref[jnp.maximum(l - 1, 0)] - h) + dn * (head_ref[after] - h)
            r = r + ru * (pltpu.roll(h, 1, 0) - h) + rd * (pltpu.roll(h, rows - 1, 0) - h)
            r = r + xl * (pltpu.roll(h, 1, 1) - h) + xr * (pltpu.roll(h, WIDE - 1, 1) - h)
            z = r * inv
            v0[l] = z
            diag_ref[l] = diag
            up_ref[l] = up * inv
            dn_ref[l] = dn * inv
            ru_ref[l] = ru * inv
            rd_ref[l] = rd * inv
            xl_ref[l] = xl * inv
            xr_ref[l] = xr * inv
            acc = acc + (r * z)[kept, 0:OWN_COLS]
        return acc

    moments = [lax.fori_loop(0, SECTIONS, faces, none)]

    for k in range(1, ITERS):
        src, dst = basis[k - 1], basis[k]

        def smooth(l, accs, src=src, dst=dst):
            v = src[l]
            new = up_ref[l] * src[jnp.maximum(l - 1, 0)] + dn_ref[l] * src[jnp.minimum(l + 1, NZ - 1)]
            new = new + ru_ref[l] * pltpu.roll(v, 1, 0) + rd_ref[l] * pltpu.roll(v, rows - 1, 0)
            new = new + xl_ref[l] * pltpu.roll(v, 1, 1) + xr_ref[l] * pltpu.roll(v, WIDE - 1, 1)
            dst[l] = new
            mine = new[kept, 0:OWN_COLS]
            scaled = mine * diag_ref[l, kept, 0:OWN_COLS]
            return accs[0] + v[kept, 0:OWN_COLS] * scaled, accs[1] + mine * scaled

        moments.extend(lax.fori_loop(0, NZ, smooth, (none, none)))

    def last(l, acc):
        block = slice(own - 8, own + OWN_ROWS)
        v = v3[l, block, :]
        mine = v[8:, 0:OWN_COLS]
        pairs = up_ref[l, kept, 0:OWN_COLS] * v3[jnp.maximum(l - 1, 0), kept, 0:OWN_COLS]
        pairs = pairs + ru_ref[l, kept, 0:OWN_COLS] * pltpu.roll(v, 1, 0)[8:, 0:OWN_COLS]
        pairs = pairs + xl_ref[l, kept, 0:OWN_COLS] * pltpu.roll(v, 1, 1)[8:, 0:OWN_COLS]
        return acc + 2.0 * mine * diag_ref[l, kept, 0:OWN_COLS] * pairs

    moments.append(lax.fori_loop(0, NZ, last, none))

    spot = lax.broadcasted_iota(jnp.int32, (8, 128), 1)
    line = jnp.zeros((8, 128), F32)
    for k, acc in enumerate(moments):
        value = jnp.sum(jnp.sum(acc, axis=0, keepdims=True), axis=1, keepdims=True)
        line = jnp.where(spot == k, value, line)
    for i in range(moments_ref.shape[0] // 8):
        moments_ref[8 * i : 8 * i + 8, :] = line


def last_kernel(sums_ref, head_ref, v0, v1, v2, v3, i0, i1, i2, out_ref):
    change = weights(sums_ref)
    own = OWN_ROWS - SPANS[2][0]
    kept = slice(own, own + OWN_ROWS)
    for l in range(NZ):
        h = head_ref[l, kept, 0:OWN_COLS]
        for c, o in zip(change, (v0, v1, v2, v3)):
            h = h + c * o[l, kept, 0:OWN_COLS]
        out_ref[l // LZ, l % LZ] = h
    for s in range(SECTIONS):
        for c, i in enumerate((i0, i1, i2)):
            out_ref[s, LZ + c] = i[s]


def shape(*dims):
    return jax.ShapeDtypeStruct(dims, F32)


def near(*dims):
    return pltpu.VMEM(dims, F32)


def call(kernel, operands, outs, scratch=(), held=()):
    operands = [pltpu.with_memory_space_constraint(x, pltpu.VMEM) if i in held else x for i, x in enumerate(operands)]
    return pl.pallas_call(
        kernel,
        out_shape=outs,
        in_specs=[VMEM] * len(operands),
        out_specs=jax.tree.map(lambda _: VMEM, outs),
        scratch_shapes=[pltpu.VMEM(dims, F32) for dims in scratch],
        compiler_params=params(),
    )(*operands)


def add_up(moments):
    return lax.all_to_all(moments, ("sec", "gx"), 0, 0, tiled=True)


def body(pressure_start, soil_type, saturated_conductivity, storage_coefficient, rainfall):
    bands = lax.axis_size("gx")
    devices = SECTIONS * bands
    packed = call(pack_kernel, (pressure_start, soil_type, rainfall), shape(SECTIONS, 9, OWN_ROWS, WIDE))
    mid = lax.all_to_all(packed, "sec", 0, 0, tiled=True)
    low = lax.ppermute(mid, "gx", [(i, i + 1) for i in range(bands - 1)])
    high = lax.ppermute(mid, "gx", [(i + 1, i) for i in range(bands - 1)])
    tables = jnp.stack([saturated_conductivity, storage_coefficient])
    tables = jnp.broadcast_to(jnp.pad(tables, ((0, 0), (0, 128 - tables.shape[1])))[:, None, :], (2, 8, 128))
    inflows = []
    state = None
    for step, (r0, r1) in enumerate(SPANS):
        rows = r1 - r0
        field = (NZ, rows, WIDE)
        wide = (NZ, FRAME, WIDE)
        outs = [near(*field)] * 5
        kernel = functools.partial(step_kernel, step, bands * OWN_ROWS)
        tail = [near(SECTIONS, OWN_ROWS, OWN_COLS), shape(devices, 128)]
        scratch = [field, field, field, (NZ + 1, rows, WIDE)] + [field] * 6 + [(SECTIONS, rows, WIDE)] * 2 + [(SECTIONS + 1, rows, WIDE)]
        if step == 0:
            outs = [near(*field), near(*wide), near(*wide), near(3, FRAME, WIDE)] + [near(*field)] * 4
            got = call(kernel, (low, mid, high, tables), outs + tail, scratch, (0, 1, 2))
            head, cond, store, rain = got[:4]
            v = got[4:8]
        else:
            got = call(kernel, (sums, head, *v, cond, store, rain), outs + tail, scratch, range(1, 9))
            head, v = got[0], got[1:5]
        inflows.append(got[-2])
        sums = add_up(got[-1])
    out = call(last_kernel, (sums, head, *v, *inflows), shape(SECTIONS, 7, OWN_ROWS, OWN_COLS), (), range(1, 9))
    out = lax.all_to_all(out, "sec", 0, 0, tiled=True)
    out = jnp.transpose(out, (1, 2, 0, 3)).reshape(7, OWN_ROWS, SECTIONS * OWN_COLS)
    return out[:LZ], out[LZ:][None]


def solution(mesh):
    placed = (P("sec", "gx", None), P("sec", "gx", None), P(), P(), P(None, "gx", None))
    return jax.shard_map(
        body,
        mesh=mesh,
        in_specs=placed,
        out_specs=(P("sec", "gx", None), P("sec", None, "gx", None)),
        check_vma=False,
    )
```

```python
import functools

import jax
import jax.numpy as jnp
from jax import lax
from jax.experimental import pallas as pl
from jax.experimental.pallas import tpu as pltpu
from jax.sharding import PartitionSpec as P

ITERS = 4
SECTIONS = 4
LZ = 4
NZ = SECTIONS * LZ
OWN_ROWS = 16
OWN_COLS = 256
WIDE = 384
HALF = 64
FRAME = 48
SPANS = ((0, 48), (0, 40), (8, 40))
WORK = ((0, 48), (8, 40), (8, 40))
F32 = jnp.float32
VMEM = pl.BlockSpec(memory_space=pltpu.VMEM)


def params():
    return pltpu.CompilerParams(vmem_limit_bytes=24 * 1024 * 1024)


def pack_kernel(head_ref, soil_ref, rain_ref, out_ref):
    section = lax.axis_index("sec")
    low_half = lax.broadcasted_iota(jnp.int32, (OWN_ROWS, 128), 1) < HALF
    rain_step = jnp.minimum(section, 2)
    for target in range(SECTIONS):
        start = target * OWN_COLS
        after = (start + OWN_COLS) % (SECTIONS * OWN_COLS)
        before = (start - 128) % (SECTIONS * OWN_COLS)

        def put(slot, read):
            out_ref[target, slot, :, 0:OWN_COLS] = read(start, OWN_COLS)
            out_ref[target, slot, :, OWN_COLS:WIDE] = jnp.where(low_half, read(after, 128), read(before, 128))

        for q in range(LZ):
            put(q, lambda at, n: head_ref[q, :, at : at + n])
            put(LZ + q, lambda at, n: soil_ref[q, :, at : at + n].astype(F32))
        put(2 * LZ, lambda at, n: rain_ref[rain_step, :, at : at + n])


def weights(sums_ref):
    total = jnp.sum(sums_ref[...], axis=0, keepdims=True)
    lane = lax.broadcasted_iota(jnp.int32, total.shape, 1)
    m = [jnp.sum(jnp.where(lane == k, total, 0.0), axis=1, keepdims=True) for k in range(8)]
    step_m = [m[k] - m[k + 1] for k in range(7)]
    zero = jnp.zeros_like(m[0])

    def form(poly, other, table):
        result = zero
        for i, a in enumerate(poly):
            for j, b in enumerate(other):
                result = result + a * b * table[i + j]
        return result

    z = [jnp.ones_like(zero)]
    direction = z
    rz = m[0]
    change = [zero] * ITERS
    for turn in range(ITERS):
        below = form(direction, direction, step_m)
        alpha = jnp.where(below > 0.0, rz / jnp.where(below > 0.0, below, 1.0), 0.0)
        for i, a in enumerate(direction):
            change[i] = change[i] + alpha * a
        if turn + 1 < ITERS:
            long = direction + [zero]
            image = [long[i] - (long[i - 1] if i else zero) for i in range(len(long))]
            z = [a - alpha * b for a, b in zip(z + [zero], image)]
            renewed = form(z, z, m)
            beta = jnp.where(rz > 0.0, renewed / jnp.where(rz > 0.0, rz, 1.0), 0.0)
            direction = [a + beta * b for a, b in zip(z, long)]
            rz = renewed
    return change


def loop(n, f, init):
    for i in range(n):
        init = f(i, init)
    return init


def recip(x):
    return pl.reciprocal(x, approx=False)


def setup_terms(h, cond_table, store_table):
    saturation = recip(1.0 + jnp.exp(-h))
    cond = cond_table * (0.05 + saturation * saturation)
    capacity = store_table * (0.1 + saturation * (1.0 - saturation))
    return saturation, cond, capacity


def gather(table, kinds):
    rows, cols = kinds.shape
    parts = []
    for j in range(cols // 128):
        parts.append(
            jnp.concatenate(
                [
                    jnp.take_along_axis(table, kinds[8 * i : 8 * i + 8, 128 * j : 128 * j + 128], axis=1, mode="promise_in_bounds")
                    for i in range(rows // 8)
                ],
                axis=0,
            )
        )
    return jnp.concatenate(parts, axis=1)


def step_kernel(step, n_rows_all, *refs):
    first = step == 0
    r0, r1 = SPANS[step]
    rows = r1 - r0
    w0, w1 = WORK[step]
    span = w1 - w0
    work = slice(w0 - r0, w1 - r0)
    own = OWN_ROWS - w0
    if first:
        (low_ref, mid_ref, high_ref, tables_ref, head_ref, cond_ref, store_ref, rain_ref) = refs[:8]
        refs = refs[8:]
    else:
        old = slice(r0 - SPANS[step - 1][0], r1 - SPANS[step - 1][0])
        old_work = slice(r0 - WORK[step - 1][0], r1 - WORK[step - 1][0])
        (sums_ref, old_head_ref, o0, o1, o2, o3, cond_ref, store_ref, rain_ref, head_ref) = refs[:10]
        old_basis = (o0, o1, o2, o3)
        refs = refs[10:]
    (v0, v1, v2, v3, inflow_ref, moments_ref) = refs[:6]
    (res_ref, cap_ref, diag_ref, up_ref, dn_ref, ru_ref, rd_ref, xl_ref, xr_ref, water_ref, low_cond_ref, flux_ref) = refs[6:]
    basis = (v0, v1, v2, v3)
    here = slice(r0, r1)
    section, band = lax.axis_index("sec"), lax.axis_index("gx")

    if first:
        for s in range(3):
            rain_ref[s, 0:16, :] = low_ref[s, 8]
            rain_ref[s, 16:32, :] = mid_ref[s, 8]
            rain_ref[s, 32:48, :] = high_ref[s, 8]
    else:
        change = weights(sums_ref)

    for s in range(SECTIONS):
        total = jnp.zeros((rows, WIDE), F32)
        for q in range(LZ):
            l = s * LZ + q
            if first:
                for part, ref in enumerate((low_ref, mid_ref, high_ref)):
                    at = slice(16 * part, 16 * part + 16)
                    kinds = ref[s, LZ + q].astype(jnp.int32)
                    head_ref[l, at, :] = ref[s, q]
                    cond_ref[l, at, :] = gather(tables_ref[0], kinds)
                    store_ref[l, at, :] = gather(tables_ref[1], kinds)
                h = head_ref[l]
            else:
                h = old_head_ref[l, old, :]
                for c, o in zip(change, old_basis):
                    h = h + c * o[l, old_work, :]
                head_ref[l] = h
            saturation, cond, capacity = setup_terms(h, cond_ref[l, here, :], store_ref[l, here, :])
            res_ref[l] = recip(cond)
            cap_ref[l] = capacity
            total = total + saturation
            if q == LZ - 1:
                low_cond_ref[s] = 0.5 * cond
        water_ref[s] = total

    flux_ref[0] = rain_ref[step, here, :]
    belows = [None] * SECTIONS
    below = None
    for s in reversed(range(SECTIONS)):
        belows[s] = below
        below = water_ref[s] if below is None else below + water_ref[s]
    for s in range(SECTIONS):
        scale = 0.5 if belows[s] is None else 0.5 + 0.5 * belows[s] / (belows[s] + 4.0)
        flux_ref[s + 1] = water_ref[s] * 0.25 * scale * flux_ref[s] + low_cond_ref[s]
        inflow_ref[s] = flux_ref[s, OWN_ROWS - r0 : 2 * OWN_ROWS - r0, 0:OWN_COLS]

    lane = lax.broadcasted_iota(jnp.int32, (span, WIDE), 1)
    col = section * OWN_COLS + lane - jnp.where(lane >= OWN_COLS + HALF, WIDE, 0)
    row = band * OWN_ROWS + (w0 - OWN_ROWS) + lax.broadcasted_iota(jnp.int32, (span, WIDE), 0)
    col_gate = jnp.where((col >= 1) & (col < SECTIONS * OWN_COLS), 2.0, 0.0).astype(F32)
    row_gate = jnp.where((row >= 1) & (row < n_rows_all), 2.0, 0.0).astype(F32)
    kept = slice(own, own + OWN_ROWS)
    none = jnp.zeros((OWN_ROWS, OWN_COLS), F32)

    def turned(x, by, axis):
        return pltpu.roll(x, by % x.shape[axis], axis)

    def faces(l, carry):
        acc, up = carry
        res = res_ref[l, work, :]
        h = head_ref[l, work, :]
        if l + 1 < NZ:
            dn = 2.0 * recip(res + res_ref[l + 1, work, :])
        else:
            dn = jnp.zeros_like(res)
        ru = row_gate * recip(res + turned(res_ref[l], 1, 0)[work])
        rd = turned(ru, -1, 0)
        xl = col_gate * recip(res + turned(res, 1, 1))
        xr = turned(xl, -1, 1)
        diag = cap_ref[l, work, :] + up + dn + ru + rd + xl + xr
        inv = recip(diag)
        r = up - dn
        if l % LZ == 0:
            r = r + flux_ref[l // LZ, work, :]
        if l % LZ == LZ - 1:
            r = r - flux_ref[l // LZ + 1, work, :]
        if l > 0:
            r = r + up * (head_ref[l - 1, work, :] - h)
        if l + 1 < NZ:
            r = r + dn * (head_ref[l + 1, work, :] - h)
        r = r + ru * (turned(head_ref[l], 1, 0)[work] - h) + rd * (turned(head_ref[l], -1, 0)[work] - h)
        r = r + xl * (turned(h, 1, 1) - h) + xr * (turned(h, -1, 1) - h)
        z = r * inv
        v0[l] = z
        diag_ref[l] = diag[kept, 0:OWN_COLS]
        if l > 0:
            up_ref[l] = up * inv
        if l + 1 < NZ:
            dn_ref[l] = dn * inv
        ru_ref[l] = ru * inv
        rd_ref[l] = rd * inv
        xl_ref[l] = xl * inv
        xr_ref[l] = xr * inv
        return acc + (r * z)[kept, 0:OWN_COLS], dn

    moments = [loop(NZ, faces, (none, jnp.zeros((span, WIDE), F32)))[0]]

    for k in range(1, ITERS):
        src, dst = basis[k - 1], basis[k]

        def smooth(l, accs):
            v = src[l]
            new = ru_ref[l] * turned(v, 1, 0) + rd_ref[l] * turned(v, -1, 0)
            new = new + xl_ref[l] * turned(v, 1, 1) + xr_ref[l] * turned(v, -1, 1)
            if l > 0:
                new = new + up_ref[l] * src[l - 1]
            if l + 1 < NZ:
                new = new + dn_ref[l] * src[l + 1]
            dst[l] = new
            mine = new[kept, 0:OWN_COLS]
            scaled = mine * diag_ref[l]
            return accs[0] + v[kept, 0:OWN_COLS] * scaled, accs[1] + mine * scaled

        moments.extend(loop(NZ, smooth, (none, none)))

    def last(l, acc):
        v = v3[l, own - 8 : own + OWN_ROWS, :]
        mine = v[8:, 0:OWN_COLS]
        pairs = ru_ref[l, kept, 0:OWN_COLS] * turned(v, 1, 0)[8:, 0:OWN_COLS]
        pairs = pairs + xl_ref[l, kept, 0:OWN_COLS] * turned(v, 1, 1)[8:, 0:OWN_COLS]
        if l > 0:
            pairs = pairs + up_ref[l, kept, 0:OWN_COLS] * v3[l - 1, kept, 0:OWN_COLS]
        return acc + 2.0 * mine * diag_ref[l] * pairs

    moments.append(loop(NZ, last, none))

    spot = lax.broadcasted_iota(jnp.int32, (8, 128), 1)
    line = jnp.zeros((8, 128), F32)
    for k, acc in enumerate(moments):
        value = jnp.sum(jnp.sum(acc, axis=0, keepdims=True), axis=1, keepdims=True)
        line = jnp.where(spot == k, value, line)
    for i in range(moments_ref.shape[0] // 8):
        moments_ref[8 * i : 8 * i + 8, :] = line


def last_kernel(sums_ref, head_ref, v0, v1, v2, v3, i0, i1, i2, out_ref):
    change = weights(sums_ref)
    own = OWN_ROWS - WORK[2][0]
    kept = slice(own, own + OWN_ROWS)
    for l in range(NZ):
        h = head_ref[l, OWN_ROWS - SPANS[2][0] : 2 * OWN_ROWS - SPANS[2][0], 0:OWN_COLS]
        for c, o in zip(change, (v0, v1, v2, v3)):
            h = h + c * o[l, kept, 0:OWN_COLS]
        out_ref[l // LZ, l % LZ] = h
    for s in range(SECTIONS):
        for c, i in enumerate((i0, i1, i2)):
            out_ref[s, LZ + c] = i[s]


def shape(*dims):
    return jax.ShapeDtypeStruct(dims, F32)


def near(*dims):
    return pltpu.VMEM(dims, F32)


def call(kernel, operands, outs, scratch=(), held=()):
    operands = [pltpu.with_memory_space_constraint(x, pltpu.VMEM) if i in held else x for i, x in enumerate(operands)]
    return pl.pallas_call(
        kernel,
        out_shape=outs,
        in_specs=[VMEM] * len(operands),
        out_specs=jax.tree.map(lambda _: VMEM, outs),
        scratch_shapes=[pltpu.VMEM(dims, F32) for dims in scratch],
        compiler_params=params(),
    )(*operands)


def add_up(moments):
    return lax.all_to_all(moments, ("sec", "gx"), 0, 0, tiled=True)


def body(pressure_start, soil_type, saturated_conductivity, storage_coefficient, rainfall):
    bands = lax.axis_size("gx")
    devices = SECTIONS * bands
    packed = call(pack_kernel, (pressure_start, soil_type, rainfall), shape(SECTIONS, 9, OWN_ROWS, WIDE))
    mid = lax.all_to_all(packed, "sec", 0, 0, tiled=True)
    low = lax.ppermute(mid, "gx", [(i, i + 1) for i in range(bands - 1)])
    high = lax.ppermute(mid, "gx", [(i + 1, i) for i in range(bands - 1)])
    tables = jnp.stack([saturated_conductivity, storage_coefficient])
    tables = jnp.broadcast_to(jnp.pad(tables, ((0, 0), (0, 128 - tables.shape[1])))[:, None, :], (2, 8, 128))
    inflows = []
    state = None
    for step, (r0, r1) in enumerate(SPANS):
        rows = r1 - r0
        field = (NZ, rows, WIDE)
        basis = (NZ, WORK[step][1] - WORK[step][0], WIDE)
        wide = (NZ, FRAME, WIDE)
        outs = [near(*field)] + [near(*basis)] * 4
        kernel = functools.partial(step_kernel, step, bands * OWN_ROWS)
        tail = [near(SECTIONS, OWN_ROWS, OWN_COLS), shape(devices, 128)]
        scratch = [field, field, (NZ, OWN_ROWS, OWN_COLS)] + [basis] * 6 + [(SECTIONS, rows, WIDE)] * 2 + [(SECTIONS + 1, rows, WIDE)]
        if step == 0:
            outs = [near(*field), near(*wide), near(*wide), near(3, FRAME, WIDE)] + [near(*basis)] * 4
            got = call(kernel, (low, mid, high, tables), outs + tail, scratch, (0, 1, 2))
            head, cond, store, rain = got[:4]
            v = got[4:8]
        else:
            got = call(kernel, (sums, head, *v, cond, store, rain), outs + tail, scratch, range(1, 9))
            head, v = got[0], got[1:5]
        inflows.append(got[-2])
        sums = add_up(got[-1])
    out = call(last_kernel, (sums, head, *v, *inflows), shape(SECTIONS, 7, OWN_ROWS, OWN_COLS), (), range(1, 9))
    out = lax.all_to_all(out, "sec", 0, 0, tiled=True)
    out = jnp.transpose(out, (1, 2, 0, 3)).reshape(7, OWN_ROWS, SECTIONS * OWN_COLS)
    return out[:LZ], out[LZ:][None]


def solution(mesh):
    placed = (P("sec", "gx", None), P("sec", "gx", None), P(), P(), P(None, "gx", None))
    return jax.shard_map(
        body,
        mesh=mesh,
        in_specs=placed,
        out_specs=(P("sec", "gx", None), P("sec", None, "gx", None)),
        check_vma=False,
    )
```

```python
import functools

import jax
import jax.numpy as jnp
from jax import lax
from jax.experimental import pallas as pl
from jax.experimental.pallas import tpu as pltpu
from jax.sharding import PartitionSpec as P

ITERS = 4
SECTIONS = 4
LZ = 4
NZ = SECTIONS * LZ
OWN_ROWS = 16
OWN_COLS = 256
WIDE = 384
HALF = 64
EDGE = 16
FRAME = 48
LOW, HIGH = 13, 12
SLOTS = 40
SPANS = ((0, 48), (0, 40), (8, 40))
WORK = ((0, 48), (8, 40), (8, 40))
F32 = jnp.float32
VMEM = pl.BlockSpec(memory_space=pltpu.VMEM)


def params():
    return pltpu.CompilerParams(vmem_limit_bytes=24 * 1024 * 1024)


def turned(x, by, axis):
    return pltpu.roll(x, by % x.shape[axis], axis)


def lanes(rows):
    return lax.broadcasted_iota(jnp.int32, (rows, 128), 1)


def tail_of(after, before):
    return jnp.where(lanes(after.shape[0]) < EDGE, after, turned(before, 2 * EDGE, 1))


def grouped(tails):
    lane = lanes(tails[0].shape[0])
    tile = tails[0]
    for j in range(1, len(tails)):
        tile = jnp.where(lane >= 2 * EDGE * j, turned(tails[j], 2 * EDGE * j, 1), tile)
    return tile


def spread(tile, j):
    tail = turned(tile, -2 * EDGE * j, 1)
    return jnp.where(lanes(tile.shape[0]) < HALF, tail, turned(tail, -2 * EDGE, 1))


def split_kernel(head_hbm, soil_hbm, out_ref, head_ref, soil_ref, sems):
    copies = [
        pltpu.make_async_copy(head_hbm, head_ref, sems.at[0]),
        pltpu.make_async_copy(soil_hbm, soil_ref, sems.at[1]),
    ]
    for copy in copies:
        copy.start()
    whole = SECTIONS * OWN_COLS
    for part, ref in enumerate((head_ref, soil_ref)):
        copies[part].wait()
        for target in range(SECTIONS):
            start = target * OWN_COLS
            after, before = (start + OWN_COLS) % whole, (start - 128) % whole
            tails = []
            for q in range(LZ):
                field = ref[q].astype(F32)
                out_ref[target, part * LZ + q] = field[:, start : start + OWN_COLS]
                tails.append(tail_of(field[:, after : after + 128], field[:, before : before + 128]))
            out_ref[target, 2 * LZ, :, 128 * part : 128 * part + 128] = grouped(tails)


def edges_kernel(mid_ref, rain_ref, low_ref, high_ref, rain_out_ref):
    section = lax.axis_index("sec")
    start = pl.multiple_of(section * OWN_COLS, OWN_COLS)
    after = pl.multiple_of(lax.rem(section + 1, SECTIONS) * OWN_COLS, OWN_COLS)
    before = pl.multiple_of(lax.rem(section + SECTIONS - 1, SECTIONS) * OWN_COLS + 128, 128)
    tails = []
    for c in range(3):
        rain_out_ref[c] = rain_ref[c, :, pl.ds(start, OWN_COLS)]
        tails.append(tail_of(rain_ref[c, :, pl.ds(after, 128)], rain_ref[c, :, pl.ds(before, 128)]))
    rain_out_ref[3] = jnp.concatenate([grouped(tails), jnp.zeros((OWN_ROWS, 128), F32)], axis=1)
    for slot in range(SLOTS):
        field = mid_ref[slot // 9, slot % 9] if slot < 36 else rain_out_ref[slot - 36]
        low_ref[LOW * slot : LOW * slot + LOW, :] = field[OWN_ROWS - LOW :]
        high_ref[HIGH * slot : HIGH * slot + HIGH, :] = field[:HIGH]


def weights(sums_ref):
    total = jnp.sum(sums_ref[...], axis=0, keepdims=True)
    lane = lax.broadcasted_iota(jnp.int32, total.shape, 1)
    m = [jnp.sum(jnp.where(lane == k, total, 0.0), axis=1, keepdims=True) for k in range(8)]
    step_m = [m[k] - m[k + 1] for k in range(7)]
    zero = jnp.zeros_like(m[0])

    def form(poly, other, table):
        result = zero
        for i, a in enumerate(poly):
            for j, b in enumerate(other):
                result = result + a * b * table[i + j]
        return result

    z = [jnp.ones_like(zero)]
    direction = z
    rz = m[0]
    change = [zero] * ITERS
    for turn in range(ITERS):
        below = form(direction, direction, step_m)
        alpha = jnp.where(below > 0.0, rz / jnp.where(below > 0.0, below, 1.0), 0.0)
        for i, a in enumerate(direction):
            change[i] = change[i] + alpha * a
        if turn + 1 < ITERS:
            long = direction + [zero]
            image = [long[i] - (long[i - 1] if i else zero) for i in range(len(long))]
            z = [a - alpha * b for a, b in zip(z + [zero], image)]
            renewed = form(z, z, m)
            beta = jnp.where(rz > 0.0, renewed / jnp.where(rz > 0.0, rz, 1.0), 0.0)
            direction = [a + beta * b for a, b in zip(z, long)]
            rz = renewed
    return change


def loop(n, f, init):
    for i in range(n):
        init = f(i, init)
    return init


def recip(x):
    return pl.reciprocal(x, approx=False)


def setup_terms(h, cond_table, store_table):
    saturation = recip(1.0 + jnp.exp(-h))
    cond = cond_table * (0.05 + saturation * saturation)
    capacity = store_table * (0.1 + saturation * (1.0 - saturation))
    return saturation, cond, capacity


def gather(table, kinds):
    rows, cols = kinds.shape
    parts = []
    for j in range(cols // 128):
        parts.append(
            jnp.concatenate(
                [
                    jnp.take_along_axis(table, kinds[8 * i : 8 * i + 8, 128 * j : 128 * j + 128], axis=1, mode="promise_in_bounds")
                    for i in range(rows // 8)
                ],
                axis=0,
            )
        )
    return jnp.concatenate(parts, axis=1)


def step_kernel(step, n_rows_all, *refs):
    first = step == 0
    r0, r1 = SPANS[step]
    rows = r1 - r0
    w0, w1 = WORK[step]
    span = w1 - w0
    work = slice(w0 - r0, w1 - r0)
    own = OWN_ROWS - w0
    if first:
        (low_ref, mid_ref, high_ref, rain_own_ref, tables_ref, head_ref, cond_ref, store_ref, rain_ref) = refs[:9]
        refs = refs[9:]
    else:
        old = slice(r0 - SPANS[step - 1][0], r1 - SPANS[step - 1][0])
        old_work = slice(r0 - WORK[step - 1][0], r1 - WORK[step - 1][0])
        (sums_ref, old_head_ref, o0, o1, o2, o3, cond_ref, store_ref, rain_ref, head_ref) = refs[:10]
        old_basis = (o0, o1, o2, o3)
        refs = refs[10:]
    (v0, v1, v2, v3, inflow_ref, moments_ref) = refs[:6]
    (res_ref, cap_ref, diag_ref, up_ref, dn_ref, ru_ref, rd_ref, xl_ref, xr_ref, water_ref, low_cond_ref, flux_ref) = refs[6:]
    basis = (v0, v1, v2, v3)
    here = slice(r0, r1)
    section, band = lax.axis_index("sec"), lax.axis_index("gx")

    if first:

        def unpack(to, slot, halo, tile, group):
            to[0:8, :] = jnp.zeros((8, WIDE), F32)
            to[FRAME - 8 : FRAME, :] = jnp.zeros((8, WIDE), F32)

            def own(slot, cols):
                return mid_ref[slot // 9, slot % 9, :, cols] if slot < 36 else rain_own_ref[slot - 36, :, cols]

            tile = slice(128 * tile, 128 * tile + 128)
            third = slice(OWN_COLS, WIDE)
            full = slice(0, OWN_COLS)
            at = slice(OWN_ROWS - LOW, OWN_ROWS)
            to[at, full] = low_ref[LOW * slot : LOW * slot + LOW, :]
            to[at, third] = spread(low_ref[LOW * halo : LOW * halo + LOW, tile], group)
            at = slice(OWN_ROWS, 2 * OWN_ROWS)
            to[at, full] = own(slot, full)
            to[at, third] = spread(own(halo, tile), group)
            at = slice(2 * OWN_ROWS, 2 * OWN_ROWS + HIGH)
            to[at, full] = high_ref[HIGH * slot : HIGH * slot + HIGH, :]
            to[at, third] = spread(high_ref[HIGH * halo : HIGH * halo + HIGH, tile], group)

        for c in range(3):
            unpack(rain_ref.at[c], 36 + c, 39, 0, c)
    else:
        change = weights(sums_ref)

    for s in range(SECTIONS):
        total = jnp.zeros((rows, WIDE), F32)
        for q in range(LZ):
            l = s * LZ + q
            if first:
                unpack(head_ref.at[l], 9 * s + q, 9 * s + 8, 0, q)
                unpack(cond_ref.at[l], 9 * s + LZ + q, 9 * s + 8, 1, q)
                kinds = cond_ref[l].astype(jnp.int32)
                cond_ref[l] = gather(tables_ref[0], kinds)
                store_ref[l] = gather(tables_ref[1], kinds)
                h = head_ref[l]
            else:
                h = old_head_ref[l, old, :]
                for c, o in zip(change, old_basis):
                    h = h + c * o[l, old_work, :]
                head_ref[l] = h
            saturation, cond, capacity = setup_terms(h, cond_ref[l, here, :], store_ref[l, here, :])
            res_ref[l] = recip(cond)
            cap_ref[l] = capacity
            total = total + saturation
            if q == LZ - 1:
                low_cond_ref[s] = 0.5 * cond
        water_ref[s] = total

    flux_ref[0] = rain_ref[step, here, :]
    belows = [None] * SECTIONS
    below = None
    for s in reversed(range(SECTIONS)):
        belows[s] = below
        below = water_ref[s] if below is None else below + water_ref[s]
    for s in range(SECTIONS):
        scale = 0.5 if belows[s] is None else 0.5 + 0.5 * belows[s] / (belows[s] + 4.0)
        flux_ref[s + 1] = water_ref[s] * 0.25 * scale * flux_ref[s] + low_cond_ref[s]
        inflow_ref[s] = flux_ref[s, OWN_ROWS - r0 : 2 * OWN_ROWS - r0, 0:OWN_COLS]

    lane = lax.broadcasted_iota(jnp.int32, (span, WIDE), 1)
    col = section * OWN_COLS + lane - jnp.where(lane >= OWN_COLS + HALF, WIDE, 0)
    row = band * OWN_ROWS + (w0 - OWN_ROWS) + lax.broadcasted_iota(jnp.int32, (span, WIDE), 0)
    col_gate = jnp.where((col >= 1) & (col < SECTIONS * OWN_COLS), 2.0, 0.0).astype(F32)
    row_gate = jnp.where((row >= 1) & (row < n_rows_all), 2.0, 0.0).astype(F32)
    kept = slice(own, own + OWN_ROWS)
    none = jnp.zeros((OWN_ROWS, OWN_COLS), F32)

    def faces(l, carry):
        acc, up = carry
        res = res_ref[l, work, :]
        h = head_ref[l, work, :]
        if l + 1 < NZ:
            dn = 2.0 * recip(res + res_ref[l + 1, work, :])
        else:
            dn = jnp.zeros_like(res)
        ru = row_gate * recip(res + turned(res_ref[l], 1, 0)[work])
        rd = turned(ru, -1, 0)
        xl = col_gate * recip(res + turned(res, 1, 1))
        xr = turned(xl, -1, 1)
        diag = cap_ref[l, work, :] + up + dn + ru + rd + xl + xr
        inv = recip(diag)
        r = up - dn
        if l % LZ == 0:
            r = r + flux_ref[l // LZ, work, :]
        if l % LZ == LZ - 1:
            r = r - flux_ref[l // LZ + 1, work, :]
        if l > 0:
            r = r + up * (head_ref[l - 1, work, :] - h)
        if l + 1 < NZ:
            r = r + dn * (head_ref[l + 1, work, :] - h)
        r = r + ru * (turned(head_ref[l], 1, 0)[work] - h) + rd * (turned(head_ref[l], -1, 0)[work] - h)
        r = r + xl * (turned(h, 1, 1) - h) + xr * (turned(h, -1, 1) - h)
        z = r * inv
        v0[l] = z
        diag_ref[l] = diag[kept, 0:OWN_COLS]
        if l > 0:
            up_ref[l] = up * inv
        if l + 1 < NZ:
            dn_ref[l] = dn * inv
        ru_ref[l] = ru * inv
        rd_ref[l] = rd * inv
        xl_ref[l] = xl * inv
        xr_ref[l] = xr * inv
        return acc + (r * z)[kept, 0:OWN_COLS], dn

    moments = [loop(NZ, faces, (none, jnp.zeros((span, WIDE), F32)))[0]]

    for k in range(1, ITERS):
        src, dst = basis[k - 1], basis[k]

        def smooth(l, accs):
            v = src[l]
            new = ru_ref[l] * turned(v, 1, 0) + rd_ref[l] * turned(v, -1, 0)
            new = new + xl_ref[l] * turned(v, 1, 1) + xr_ref[l] * turned(v, -1, 1)
            if l > 0:
                new = new + up_ref[l] * src[l - 1]
            if l + 1 < NZ:
                new = new + dn_ref[l] * src[l + 1]
            dst[l] = new
            mine = new[kept, 0:OWN_COLS]
            scaled = mine * diag_ref[l]
            return accs[0] + v[kept, 0:OWN_COLS] * scaled, accs[1] + mine * scaled

        moments.extend(loop(NZ, smooth, (none, none)))

    def last(l, acc):
        v = v3[l, own - 8 : own + OWN_ROWS, :]
        mine = v[8:, 0:OWN_COLS]
        pairs = ru_ref[l, kept, 0:OWN_COLS] * turned(v, 1, 0)[8:, 0:OWN_COLS]
        pairs = pairs + xl_ref[l, kept, 0:OWN_COLS] * turned(v, 1, 1)[8:, 0:OWN_COLS]
        if l > 0:
            pairs = pairs + up_ref[l, kept, 0:OWN_COLS] * v3[l - 1, kept, 0:OWN_COLS]
        return acc + 2.0 * mine * diag_ref[l] * pairs

    moments.append(loop(NZ, last, none))

    spot = lax.broadcasted_iota(jnp.int32, (8, 128), 1)
    line = jnp.zeros((8, 128), F32)
    for k, acc in enumerate(moments):
        value = jnp.sum(jnp.sum(acc, axis=0, keepdims=True), axis=1, keepdims=True)
        line = jnp.where(spot == k, value, line)
    for i in range(moments_ref.shape[0] // 8):
        moments_ref[8 * i : 8 * i + 8, :] = line


def last_kernel(sums_ref, head_ref, v0, v1, v2, v3, i0, i1, i2, out_ref):
    change = weights(sums_ref)
    own = OWN_ROWS - WORK[2][0]
    kept = slice(own, own + OWN_ROWS)
    for l in range(NZ):
        h = head_ref[l, OWN_ROWS - SPANS[2][0] : 2 * OWN_ROWS - SPANS[2][0], 0:OWN_COLS]
        for c, o in zip(change, (v0, v1, v2, v3)):
            h = h + c * o[l, kept, 0:OWN_COLS]
        out_ref[l // LZ, l % LZ] = h
    for s in range(SECTIONS):
        for c, i in enumerate((i0, i1, i2)):
            out_ref[s, LZ + c] = i[s]


def shape(*dims):
    return jax.ShapeDtypeStruct(dims, F32)


def near(*dims):
    return pltpu.VMEM(dims, F32)


def held(*arrays, space=pltpu.VMEM):
    return tuple(pltpu.with_memory_space_constraint(x, space) for x in arrays)


def call(kernel, operands, outs, scratch=(), in_specs=None, out_specs=None):
    return pl.pallas_call(
        kernel,
        out_shape=outs,
        in_specs=in_specs or [VMEM] * len(operands),
        out_specs=out_specs or jax.tree.map(lambda _: VMEM, outs),
        scratch_shapes=[pltpu.VMEM(dims, F32) if isinstance(dims, tuple) else dims for dims in scratch],
        compiler_params=params(),
    )(*operands)


def join_kernel(parts_ref, head_hbm, flows_hbm, sems):
    copies = []
    for t in range(SECTIONS):
        cols = slice(t * OWN_COLS, (t + 1) * OWN_COLS)
        copies.append(pltpu.make_async_copy(parts_ref.at[t, 0:LZ], head_hbm.at[:, :, cols], sems.at[0, t]))
        copies.append(pltpu.make_async_copy(parts_ref.at[t, LZ : LZ + 3], flows_hbm.at[0, :, :, cols], sems.at[1, t]))
    for copy in copies:
        copy.start()
    for copy in copies:
        copy.wait()


def add_up(moments):
    return lax.all_to_all(moments, ("sec", "gx"), 0, 0, tiled=True)


def body(pressure_start, soil_type, saturated_conductivity, storage_coefficient, rainfall):
    bands = lax.axis_size("gx")
    devices = SECTIONS * bands
    outside = pl.BlockSpec(memory_space=pl.ANY)
    block = (LZ, OWN_ROWS, SECTIONS * OWN_COLS)
    packed = call(
        split_kernel,
        held(pressure_start, soil_type, space=pltpu.HBM),
        near(SECTIONS, 9, OWN_ROWS, OWN_COLS),
        (block, pltpu.VMEM(block, jnp.int32), pltpu.SemaphoreType.DMA((2,))),
        in_specs=[outside] * 2,
    )
    mid = lax.all_to_all(packed, "sec", 0, 0, tiled=True)
    to_low, to_high, rain_own = call(
        edges_kernel,
        held(mid, rainfall),
        [near(LOW * SLOTS, OWN_COLS), near(HIGH * SLOTS, OWN_COLS), near(4, OWN_ROWS, OWN_COLS)],
    )
    low = lax.ppermute(to_low, "gx", [(i, i + 1) for i in range(bands - 1)])
    high = lax.ppermute(to_high, "gx", [(i + 1, i) for i in range(bands - 1)])
    tables = jnp.stack([saturated_conductivity, storage_coefficient])
    tables = jnp.broadcast_to(jnp.pad(tables, ((0, 0), (0, 128 - tables.shape[1])))[:, None, :], (2, 8, 128))
    inflows = []
    state = None
    for step, (r0, r1) in enumerate(SPANS):
        rows = r1 - r0
        field = (NZ, rows, WIDE)
        basis = (NZ, WORK[step][1] - WORK[step][0], WIDE)
        wide = (NZ, FRAME, WIDE)
        outs = [near(*field)] + [near(*basis)] * 4
        kernel = functools.partial(step_kernel, step, bands * OWN_ROWS)
        tail = [near(SECTIONS, OWN_ROWS, OWN_COLS), shape(devices, 128)]
        scratch = [field, field, (NZ, OWN_ROWS, OWN_COLS)] + [basis] * 6 + [(SECTIONS, rows, WIDE)] * 2 + [(SECTIONS + 1, rows, WIDE)]
        if step == 0:
            outs = [near(*field), near(*wide), near(*wide), near(3, FRAME, WIDE)] + [near(*basis)] * 4
            got = call(kernel, (*held(low, mid, high, rain_own), tables), outs + tail, scratch)
            head, cond, store, rain = got[:4]
            v = got[4:8]
        else:
            got = call(kernel, (sums, *held(head, *v, cond, store, rain)), outs + tail, scratch)
            head, v = got[0], got[1:5]
        inflows.append(got[-2])
        sums = add_up(got[-1])
    out = call(last_kernel, (sums, *held(head, *v, *inflows)), near(SECTIONS, 7, OWN_ROWS, OWN_COLS))
    out = lax.all_to_all(out, "sec", 0, 0, tiled=True)
    return call(
        join_kernel,
        held(out),
        [shape(*block), shape(1, 3, *block[1:])],
        (pltpu.SemaphoreType.DMA((2, SECTIONS)),),
        out_specs=[outside] * 2,
    )


def solution(mesh):
    placed = (P("sec", "gx", None), P("sec", "gx", None), P(), P(), P(None, "gx", None))
    return jax.shard_map(
        body,
        mesh=mesh,
        in_specs=placed,
        out_specs=(P("sec", "gx", None), P("sec", None, "gx", None)),
        check_vma=False,
    )
```

```python
import functools

import jax
import jax.numpy as jnp
from jax import lax
from jax.experimental import pallas as pl
from jax.experimental.pallas import tpu as pltpu
from jax.sharding import PartitionSpec as P

ITERS = 4
SECTIONS = 4
LZ = 4
NZ = SECTIONS * LZ
OWN_ROWS = 16
OWN_COLS = 256
WIDE = 384
HALF = 64
EDGE = 16
FRAME = 48
SLOTS = 40
SPANS = ((0, 48), (0, 40), (8, 40))
WORK = ((0, 48), (8, 40), (8, 40))
F32 = jnp.float32
VMEM = pl.BlockSpec(memory_space=pltpu.VMEM)


def params():
    return pltpu.CompilerParams(vmem_limit_bytes=24 * 1024 * 1024)


def turned(x, by, axis):
    return pltpu.roll(x, by % x.shape[axis], axis)


def lanes(rows):
    return lax.broadcasted_iota(jnp.int32, (rows, 128), 1)


def tail_of(after, before):
    return jnp.where(lanes(after.shape[0]) < EDGE, after, turned(before, 2 * EDGE, 1))


def grouped(tails):
    lane = lanes(tails[0].shape[0])
    tile = tails[0]
    for j in range(1, len(tails)):
        tile = jnp.where(lane >= 2 * EDGE * j, turned(tails[j], 2 * EDGE * j, 1), tile)
    return tile


def spread(tile, count):
    for _ in range(count):
        later = turned(tile, -2 * EDGE, 1)
        yield jnp.where(lanes(tile.shape[0]) < HALF, tile, later)
        tile = later


def split_kernel(head_hbm, soil_hbm, out_ref, head_ref, soil_ref, sems):
    copies = [
        pltpu.make_async_copy(head_hbm, head_ref, sems.at[0]),
        pltpu.make_async_copy(soil_hbm, soil_ref, sems.at[1]),
    ]
    for copy in copies:
        copy.start()
    whole = SECTIONS * OWN_COLS
    for part, ref in enumerate((head_ref, soil_ref)):
        copies[part].wait()
        for target in range(SECTIONS):
            start = target * OWN_COLS
            after, before = (start + OWN_COLS) % whole, (start - 128) % whole
            tails = []
            for q in range(LZ):
                field = ref[q].astype(F32)
                out_ref[target, part * LZ + q] = field[:, start : start + OWN_COLS]
                tails.append(tail_of(field[:, after : after + 128], field[:, before : before + 128]))
            out_ref[target, 2 * LZ, :, 128 * part : 128 * part + 128] = grouped(tails)


def edges_kernel(mid_ref, rain_ref, out_ref):
    section = lax.axis_index("sec")
    start = pl.multiple_of(section * OWN_COLS, OWN_COLS)
    after = pl.multiple_of(lax.rem(section + 1, SECTIONS) * OWN_COLS, OWN_COLS)
    before = pl.multiple_of(lax.rem(section + SECTIONS - 1, SECTIONS) * OWN_COLS + 128, 128)
    tails = []
    for c in range(3):
        out_ref[36 + c] = rain_ref[c, :, pl.ds(start, OWN_COLS)]
        tails.append(tail_of(rain_ref[c, :, pl.ds(after, 128)], rain_ref[c, :, pl.ds(before, 128)]))
    out_ref[39] = jnp.concatenate([grouped(tails), jnp.zeros((OWN_ROWS, 128), F32)], axis=1)
    for slot in range(36):
        out_ref[slot] = mid_ref[slot // 9, slot % 9]


def weights(sums_ref):
    total = jnp.sum(sums_ref[...], axis=0, keepdims=True)
    lane = lax.broadcasted_iota(jnp.int32, total.shape, 1)
    m = [jnp.sum(jnp.where(lane == k, total, 0.0), axis=1, keepdims=True) for k in range(8)]
    step_m = [m[k] - m[k + 1] for k in range(7)]
    zero = jnp.zeros_like(m[0])

    def form(poly, other, table):
        result = zero
        for i, a in enumerate(poly):
            for j, b in enumerate(other):
                result = result + a * b * table[i + j]
        return result

    z = [jnp.ones_like(zero)]
    direction = z
    rz = m[0]
    change = [zero] * ITERS
    for turn in range(ITERS):
        below = form(direction, direction, step_m)
        alpha = jnp.where(below > 0.0, rz / jnp.where(below > 0.0, below, 1.0), 0.0)
        for i, a in enumerate(direction):
            change[i] = change[i] + alpha * a
        if turn + 1 < ITERS:
            long = direction + [zero]
            image = [long[i] - (long[i - 1] if i else zero) for i in range(len(long))]
            z = [a - alpha * b for a, b in zip(z + [zero], image)]
            renewed = form(z, z, m)
            beta = jnp.where(rz > 0.0, renewed / jnp.where(rz > 0.0, rz, 1.0), 0.0)
            direction = [a + beta * b for a, b in zip(z, long)]
            rz = renewed
    return change


def loop(n, f, init):
    for i in range(n):
        init = f(i, init)
    return init


def recip(x):
    return pl.reciprocal(x, approx=False)


def setup_terms(h, cond_table, store_table):
    saturation = recip(1.0 + jnp.exp(-h))
    cond = cond_table * (0.05 + saturation * saturation)
    capacity = store_table * (0.1 + saturation * (1.0 - saturation))
    return saturation, cond, capacity


def gather(table, kinds):
    rows, cols = kinds.shape
    parts = []
    for j in range(cols // 128):
        parts.append(
            jnp.concatenate(
                [
                    jnp.take_along_axis(table, kinds[8 * i : 8 * i + 8, 128 * j : 128 * j + 128], axis=1, mode="promise_in_bounds")
                    for i in range(rows // 8)
                ],
                axis=0,
            )
        )
    return jnp.concatenate(parts, axis=1)


def enter_kernel(from_ref, tables_ref, head_ref, cond_ref, store_ref, res_ref, cap_ref, rain_ref, water_ref, low_cond_ref):
    packs = [(rain_ref, 0, 36, 39, 0, 3)]
    for s in range(SECTIONS):
        packs.append((head_ref, s * LZ, 9 * s, 9 * s + 8, 0, LZ))
        packs.append((cond_ref, s * LZ, 9 * s + LZ, 9 * s + 8, 1, LZ))
    for ref, first, slot, halo, tile, count in packs:
        for q, third in enumerate(spread(from_ref[halo, :, 128 * tile : 128 * tile + 128], count)):
            ref[first + q, :, 0:OWN_COLS] = from_ref[slot + q]
            ref[first + q, :, OWN_COLS:WIDE] = third
    for l in range(NZ):
        store_ref[l] = gather(tables_ref[1], cond_ref[l].astype(jnp.int32))
    for l in range(NZ):
        cond_ref[l] = gather(tables_ref[0], cond_ref[l].astype(jnp.int32))
    for s in range(SECTIONS):
        total = jnp.zeros((OWN_ROWS, WIDE), F32)
        for q in range(LZ):
            l = s * LZ + q
            saturation, cond, capacity = setup_terms(head_ref[l], cond_ref[l], store_ref[l])
            res_ref[l] = recip(cond)
            cap_ref[l] = capacity
            total = total + saturation
        water_ref[s] = total
        low_cond_ref[s] = 0.5 * cond


def framed(parts, start, stop):
    def read(l):
        pieces = []
        for at, ref in enumerate(parts):
            lo, hi = max(start - 16 * at, 0), min(stop - 16 * at, 16)
            if lo < hi:
                pieces.append(ref[l, lo:hi, :])
        return jnp.concatenate(pieces, axis=0)

    return read


def step_kernel(step, n_rows_all, *refs):
    first = step == 0
    r0, r1 = SPANS[step]
    rows = r1 - r0
    w0, w1 = WORK[step]
    span = w1 - w0
    work = slice(w0 - r0, w1 - r0)
    own = OWN_ROWS - w0
    refs = list(refs)

    def take(n):
        taken, refs[:n] = refs[:n], []
        return taken

    def take_framed(n):
        low, mid, high = take(n), take(n), take(n)
        return [framed(parts, r0, r1) for parts in zip(low, mid, high)]

    if first:
        head, res, cap, rain, water, low_cond = take_framed(6)
    else:
        (sums_ref,) = take(1)
        old_basis = take(ITERS)
        old_work = slice(r0 - WORK[step - 1][0], r1 - WORK[step - 1][0])
        if step == 1:
            old_head, cond_of, store_of, rain = take_framed(4)
        else:
            (old_head_ref,) = take(1)
            old = slice(r0 - SPANS[step - 1][0], r1 - SPANS[step - 1][0])
            old_head = lambda l: old_head_ref[l, old, :]
            cond_of, store_of, rain = take_framed(3)
        (head_ref,) = take(1)
    v0, v1, v2, v3, inflow_ref, moments_ref = take(6)
    diag_ref, up_ref, dn_ref, ru_ref, rd_ref, xl_ref, xr_ref, flux_ref = take(8)
    if not first:
        res_ref, cap_ref, water_ref, low_cond_ref = take(4)
        head, res, cap, water, low_cond = [
            (lambda l, ref=ref: ref[l]) for ref in (head_ref, res_ref, cap_ref, water_ref, low_cond_ref)
        ]
    basis = (v0, v1, v2, v3)
    section = lax.axis_index("sec")
    band = lax.axis_index("pair") * 2 + lax.axis_index("core")

    if not first:
        change = weights(sums_ref)
        for s in range(SECTIONS):
            total = jnp.zeros((rows, WIDE), F32)
            for q in range(LZ):
                l = s * LZ + q
                h = old_head(l)
                for c, o in zip(change, old_basis):
                    h = h + c * o[l, old_work, :]
                head_ref[l] = h
                saturation, cond, capacity = setup_terms(h, cond_of(l), store_of(l))
                res_ref[l] = recip(cond)
                cap_ref[l] = capacity
                total = total + saturation
            water_ref[s] = total
            low_cond_ref[s] = 0.5 * cond

    flux_ref[0] = rain(step)
    belows = [None] * SECTIONS
    below = None
    for s in reversed(range(SECTIONS)):
        belows[s] = below
        below = water(s) if below is None else below + water(s)
    for s in range(SECTIONS):
        scale = 0.5 if belows[s] is None else 0.5 + 0.5 * belows[s] / (belows[s] + 4.0)
        flux_ref[s + 1] = water(s) * 0.25 * scale * flux_ref[s] + low_cond(s)
        inflow_ref[s] = flux_ref[s, OWN_ROWS - r0 : 2 * OWN_ROWS - r0, 0:OWN_COLS]

    lane = lax.broadcasted_iota(jnp.int32, (span, WIDE), 1)
    col = section * OWN_COLS + lane - jnp.where(lane >= OWN_COLS + HALF, WIDE, 0)
    row = band * OWN_ROWS + (w0 - OWN_ROWS) + lax.broadcasted_iota(jnp.int32, (span, WIDE), 0)
    col_gate = jnp.where((col >= 1) & (col < SECTIONS * OWN_COLS), 2.0, 0.0).astype(F32)
    row_gate = jnp.where((row >= 1) & (row < n_rows_all), 2.0, 0.0).astype(F32)
    kept = slice(own, own + OWN_ROWS)
    none = jnp.zeros((OWN_ROWS, OWN_COLS), F32)

    def faces(l, carry):
        acc, up = carry
        around, tops = res(l), head(l)
        mine, h = around[work], tops[work]
        if l + 1 < NZ:
            dn = 2.0 * recip(mine + res(l + 1)[work])
        else:
            dn = jnp.zeros_like(mine)
        ru = row_gate * recip(mine + turned(around, 1, 0)[work])
        rd = turned(ru, -1, 0)
        xl = col_gate * recip(mine + turned(mine, 1, 1))
        xr = turned(xl, -1, 1)
        diag = cap(l)[work] + up + dn + ru + rd + xl + xr
        inv = recip(diag)
        r = up - dn
        if l % LZ == 0:
            r = r + flux_ref[l // LZ, work, :]
        if l % LZ == LZ - 1:
            r = r - flux_ref[l // LZ + 1, work, :]
        if l > 0:
            r = r + up * (head(l - 1)[work] - h)
        if l + 1 < NZ:
            r = r + dn * (head(l + 1)[work] - h)
        r = r + ru * (turned(tops, 1, 0)[work] - h) + rd * (turned(tops, -1, 0)[work] - h)
        r = r + xl * (turned(h, 1, 1) - h) + xr * (turned(h, -1, 1) - h)
        z = r * inv
        v0[l] = z
        diag_ref[l] = diag[kept, 0:OWN_COLS]
        if l > 0:
            up_ref[l] = up * inv
        if l + 1 < NZ:
            dn_ref[l] = dn * inv
        ru_ref[l] = ru * inv
        rd_ref[l] = rd * inv
        xl_ref[l] = xl * inv
        xr_ref[l] = xr * inv
        return acc + (r * z)[kept, 0:OWN_COLS], dn

    moments = [loop(NZ, faces, (none, jnp.zeros((span, WIDE), F32)))[0]]

    for k in range(1, ITERS):
        src, dst = basis[k - 1], basis[k]

        def smooth(l, accs):
            v = src[l]
            new = ru_ref[l] * turned(v, 1, 0) + rd_ref[l] * turned(v, -1, 0)
            new = new + xl_ref[l] * turned(v, 1, 1) + xr_ref[l] * turned(v, -1, 1)
            if l > 0:
                new = new + up_ref[l] * src[l - 1]
            if l + 1 < NZ:
                new = new + dn_ref[l] * src[l + 1]
            dst[l] = new
            mine = new[kept, 0:OWN_COLS]
            scaled = mine * diag_ref[l]
            return accs[0] + v[kept, 0:OWN_COLS] * scaled, accs[1] + mine * scaled

        moments.extend(loop(NZ, smooth, (none, none)))

    def last(l, acc):
        v = v3[l, own - 8 : own + OWN_ROWS, :]
        mine = v[8:, 0:OWN_COLS]
        pairs = ru_ref[l, kept, 0:OWN_COLS] * turned(v, 1, 0)[8:, 0:OWN_COLS]
        pairs = pairs + xl_ref[l, kept, 0:OWN_COLS] * turned(v, 1, 1)[8:, 0:OWN_COLS]
        if l > 0:
            pairs = pairs + up_ref[l, kept, 0:OWN_COLS] * v3[l - 1, kept, 0:OWN_COLS]
        return acc + 2.0 * mine * diag_ref[l] * pairs

    moments.append(loop(NZ, last, none))

    spot = lax.broadcasted_iota(jnp.int32, (8, 128), 1)
    line = jnp.zeros((8, 128), F32)
    for k, acc in enumerate(moments):
        value = jnp.sum(jnp.sum(acc, axis=0, keepdims=True), axis=1, keepdims=True)
        line = jnp.where(spot == k, value, line)
    moments_ref[...] = line


def last_kernel(sums_ref, head_ref, v0, v1, v2, v3, i0, i1, i2, out_ref):
    change = weights(sums_ref)
    own = OWN_ROWS - WORK[2][0]
    kept = slice(own, own + OWN_ROWS)
    for l in range(NZ):
        h = head_ref[l, OWN_ROWS - SPANS[2][0] : 2 * OWN_ROWS - SPANS[2][0], 0:OWN_COLS]
        for c, o in zip(change, (v0, v1, v2, v3)):
            h = h + c * o[l, kept, 0:OWN_COLS]
        out_ref[l // LZ, l % LZ] = h
    for s in range(SECTIONS):
        for c, i in enumerate((i0, i1, i2)):
            out_ref[s, LZ + c] = i[s]


def shape(*dims):
    return jax.ShapeDtypeStruct(dims, F32)


def near(*dims):
    return pltpu.VMEM(dims, F32)


def held(*arrays, space=pltpu.VMEM):
    return tuple(pltpu.with_memory_space_constraint(x, space) for x in arrays)


def call(kernel, operands, outs, scratch=(), in_specs=None, out_specs=None, **more):
    return pl.pallas_call(
        kernel,
        **more,
        out_shape=outs,
        in_specs=in_specs or [VMEM] * len(operands),
        out_specs=out_specs or jax.tree.map(lambda _: VMEM, outs),
        scratch_shapes=[pltpu.VMEM(dims, F32) if isinstance(dims, tuple) else dims for dims in scratch],
        compiler_params=params(),
    )(*operands)


def join_kernel(parts_ref, head_hbm, flows_hbm, sems):
    copies = []
    for t in range(SECTIONS):
        cols = slice(t * OWN_COLS, (t + 1) * OWN_COLS)
        copies.append(pltpu.make_async_copy(parts_ref.at[t, 0:LZ], head_hbm.at[:, :, cols], sems.at[0, t]))
        copies.append(pltpu.make_async_copy(parts_ref.at[t, LZ : LZ + 3], flows_hbm.at[0, :, :, cols], sems.at[1, t]))
    for copy in copies:
        copy.start()
    for copy in copies:
        copy.wait()


def add_up(moments):
    chips = SECTIONS * lax.axis_size("pair")
    both = moments + lax.ppermute(moments, "core", [(0, 1), (1, 0)])
    rows = lax.all_to_all(jnp.broadcast_to(both[:1, None], (chips, 1, 128)), ("sec", "pair"), 0, 0, tiled=True)
    return rows.reshape(chips, 128)


def body(pressure_start, soil_type, saturated_conductivity, storage_coefficient, rainfall):
    gx = ("pair", "core")
    bands = 2 * lax.axis_size("pair")
    outside = pl.BlockSpec(memory_space=pl.ANY)
    block = (LZ, OWN_ROWS, SECTIONS * OWN_COLS)
    packed = call(
        split_kernel,
        held(pressure_start, soil_type, space=pltpu.HBM),
        near(SECTIONS, 9, OWN_ROWS, OWN_COLS),
        (block, pltpu.VMEM(block, jnp.int32), pltpu.SemaphoreType.DMA((2,))),
        in_specs=[outside] * 2,
    )
    mid = lax.all_to_all(packed, "sec", 0, 0, tiled=True)
    to_send = call(edges_kernel, held(mid, rainfall), near(SLOTS, OWN_ROWS, OWN_COLS))
    low = lax.ppermute(to_send, gx, [(i, i + 1) for i in range(bands - 1)])
    high = lax.ppermute(to_send, gx, [(i + 1, i) for i in range(bands - 1)])
    tables = jnp.stack([saturated_conductivity, storage_coefficient])
    tables = jnp.broadcast_to(jnp.pad(tables, ((0, 0), (0, 128 - tables.shape[1])))[:, None, :], (2, 8, 128))

    def entered(rows_sent):
        return call(
            enter_kernel,
            (*held(rows_sent), tables),
            [near(n, OWN_ROWS, WIDE) for n in (NZ,) * 5 + (3,) + (SECTIONS,) * 2],
            cost_estimate=pl.CostEstimate(flops=10_000_000, bytes_accessed=4_000_000, transcendentals=300_000),
        )

    parts = [entered(low), entered(to_send), entered(high)]

    def pick(*which):
        return [part[k] for part in parts for k in which]

    inflows = []
    state = None
    for step, (r0, r1) in enumerate(SPANS):
        rows = r1 - r0
        field = (NZ, rows, WIDE)
        basis = (NZ, WORK[step][1] - WORK[step][0], WIDE)
        outs = [near(*field)] + [near(*basis)] * 4
        kernel = functools.partial(step_kernel, step, bands * OWN_ROWS)
        tail = [near(SECTIONS, OWN_ROWS, OWN_COLS), near(8, 128)]
        scratch = [(NZ, OWN_ROWS, OWN_COLS)] + [basis] * 6 + [(SECTIONS + 1, rows, WIDE)]
        if step == 0:
            got = call(kernel, held(*pick(0, 3, 4, 5, 6, 7)), [near(*basis)] * 4 + tail, scratch)
            v = got[:4]
        else:
            state = pick(0, 1, 2, 5) if step == 1 else [head, *pick(1, 2, 5)]
            soil = [field] * 2 + [(SECTIONS, rows, WIDE)] * 2
            got = call(kernel, (sums, *held(*v, *state)), outs + tail, scratch + soil)
            head, v = got[0], got[1:5]
        inflows.append(got[-2])
        sums = add_up(got[-1])
    out = call(last_kernel, (sums, *held(head, *v, *inflows)), near(SECTIONS, 7, OWN_ROWS, OWN_COLS))
    out = lax.all_to_all(out, "sec", 0, 0, tiled=True)
    return call(
        join_kernel,
        held(out),
        [shape(*block), shape(1, 3, *block[1:])],
        (pltpu.SemaphoreType.DMA((2, SECTIONS)),),
        out_specs=[outside] * 2,
    )


def solution(mesh):
    sections, bands = mesh.devices.shape
    gx = ("pair", "core")
    placed = (P("sec", gx, None), P("sec", gx, None), P(), P(), P(None, gx, None))
    return jax.shard_map(
        body,
        mesh=jax.sharding.Mesh(mesh.devices.reshape(sections, bands // 2, 2), ("sec", *gx)),
        in_specs=placed,
        out_specs=(P("sec", gx, None), P("sec", None, gx, None)),
        check_vma=False,
    )
```

```python
import functools

import jax
import jax.numpy as jnp
from jax import lax
from jax.experimental import pallas as pl
from jax.experimental.pallas import tpu as pltpu
from jax.sharding import PartitionSpec as P

ITERS = 4
SECTIONS = 4
LZ = 4
NZ = SECTIONS * LZ
OWN_ROWS = 16
OWN_COLS = 256
WIDE = 384
HALF = 64
EDGE = 16
FRAME = 48
SLOTS = 40
SPANS = ((0, 48), (0, 40), (8, 40))
WORK = ((0, 48), (8, 40), (8, 40))
F32 = jnp.float32
VMEM = pl.BlockSpec(memory_space=pltpu.VMEM)


def params():
    return pltpu.CompilerParams(vmem_limit_bytes=24 * 1024 * 1024)


def turned(x, by, axis):
    return pltpu.roll(x, by % x.shape[axis], axis)


def lanes(rows):
    return lax.broadcasted_iota(jnp.int32, (rows, 128), 1)


def tail_of(after, before):
    return jnp.where(lanes(after.shape[0]) < EDGE, after, turned(before, 2 * EDGE, 1))


def grouped(tails):
    lane = lanes(tails[0].shape[0])
    tile = tails[0]
    for j in range(1, len(tails)):
        tile = jnp.where(lane >= 2 * EDGE * j, turned(tails[j], 2 * EDGE * j, 1), tile)
    return tile


def spread(tile, count):
    for _ in range(count):
        later = turned(tile, -2 * EDGE, 1)
        yield jnp.where(lanes(tile.shape[0]) < HALF, tile, later)
        tile = later


def split_kernel(head_hbm, soil_hbm, out_ref, head_ref, soil_ref, sems):
    copies = [
        pltpu.make_async_copy(head_hbm, head_ref, sems.at[0]),
        pltpu.make_async_copy(soil_hbm, soil_ref, sems.at[1]),
    ]
    for copy in copies:
        copy.start()
    whole = SECTIONS * OWN_COLS
    for part, ref in enumerate((head_ref, soil_ref)):
        copies[part].wait()
        for target in range(SECTIONS):
            start = target * OWN_COLS
            after, before = (start + OWN_COLS) % whole, (start - 128) % whole
            tails = []
            for q in range(LZ):
                field = ref[q].astype(F32)
                out_ref[target, part * LZ + q] = field[:, start : start + OWN_COLS]
                tails.append(tail_of(field[:, after : after + 128], field[:, before : before + 128]))
            out_ref[target, 2 * LZ, :, 128 * part : 128 * part + 128] = grouped(tails)


def edges_kernel(mid_ref, rain_ref, out_ref):
    section = lax.axis_index("sec")
    start = pl.multiple_of(section * OWN_COLS, OWN_COLS)
    after = pl.multiple_of(lax.rem(section + 1, SECTIONS) * OWN_COLS, OWN_COLS)
    before = pl.multiple_of(lax.rem(section + SECTIONS - 1, SECTIONS) * OWN_COLS + 128, 128)
    tails = []
    for c in range(3):
        out_ref[36 + c] = rain_ref[c, :, pl.ds(start, OWN_COLS)]
        tails.append(tail_of(rain_ref[c, :, pl.ds(after, 128)], rain_ref[c, :, pl.ds(before, 128)]))
    out_ref[39] = jnp.concatenate([grouped(tails), jnp.zeros((OWN_ROWS, 128), F32)], axis=1)
    for slot in range(36):
        out_ref[slot] = mid_ref[slot // 9, slot % 9]


def weights(sums_ref):
    total = jnp.sum(sums_ref[...], axis=0, keepdims=True)
    lane = lax.broadcasted_iota(jnp.int32, total.shape, 1)
    m = [jnp.sum(jnp.where(lane == k, total, 0.0), axis=1, keepdims=True) for k in range(8)]
    step_m = [m[k] - m[k + 1] for k in range(7)]
    zero = jnp.zeros_like(m[0])

    def form(poly, other, table):
        result = zero
        for i, a in enumerate(poly):
            for j, b in enumerate(other):
                result = result + a * b * table[i + j]
        return result

    z = [jnp.ones_like(zero)]
    direction = z
    rz = m[0]
    change = [zero] * ITERS
    for turn in range(ITERS):
        below = form(direction, direction, step_m)
        alpha = jnp.where(below > 0.0, rz / jnp.where(below > 0.0, below, 1.0), 0.0)
        for i, a in enumerate(direction):
            change[i] = change[i] + alpha * a
        if turn + 1 < ITERS:
            long = direction + [zero]
            image = [long[i] - (long[i - 1] if i else zero) for i in range(len(long))]
            z = [a - alpha * b for a, b in zip(z + [zero], image)]
            renewed = form(z, z, m)
            beta = jnp.where(rz > 0.0, renewed / jnp.where(rz > 0.0, rz, 1.0), 0.0)
            direction = [a + beta * b for a, b in zip(z, long)]
            rz = renewed
    return change


def loop(n, f, init):
    for i in range(n):
        init = f(i, init)
    return init


def recip(x):
    return pl.reciprocal(x, approx=False)


def setup_terms(h, cond_table, store_table):
    saturation = recip(1.0 + jnp.exp(-h))
    cond = cond_table * (0.05 + saturation * saturation)
    capacity = store_table * (0.1 + saturation * (1.0 - saturation))
    return saturation, cond, capacity


def gather(table, kinds):
    rows, cols = kinds.shape
    parts = []
    for j in range(cols // 128):
        parts.append(
            jnp.concatenate(
                [
                    jnp.take_along_axis(table, kinds[8 * i : 8 * i + 8, 128 * j : 128 * j + 128], axis=1, mode="promise_in_bounds")
                    for i in range(rows // 8)
                ],
                axis=0,
            )
        )
    return jnp.concatenate(parts, axis=1)


def enter_kernel(from_ref, tables_ref, head_ref, cond_ref, store_ref, res_ref, cap_ref, rain_ref, water_ref, low_cond_ref):
    packs = [(rain_ref, 0, 36, 39, 0, 3)]
    for s in range(SECTIONS):
        packs.append((head_ref, s * LZ, 9 * s, 9 * s + 8, 0, LZ))
        packs.append((cond_ref, s * LZ, 9 * s + LZ, 9 * s + 8, 1, LZ))
    for ref, first, slot, halo, tile, count in packs:
        for q, third in enumerate(spread(from_ref[halo, :, 128 * tile : 128 * tile + 128], count)):
            ref[first + q, :, 0:OWN_COLS] = from_ref[slot + q]
            ref[first + q, :, OWN_COLS:WIDE] = third
    for l in range(NZ):
        store_ref[l] = gather(tables_ref[1], cond_ref[l].astype(jnp.int32))
    for l in range(NZ):
        cond_ref[l] = gather(tables_ref[0], cond_ref[l].astype(jnp.int32))
    for s in range(SECTIONS):
        total = jnp.zeros((OWN_ROWS, WIDE), F32)
        for q in range(LZ):
            l = s * LZ + q
            saturation, cond, capacity = setup_terms(head_ref[l], cond_ref[l], store_ref[l])
            res_ref[l] = recip(cond)
            cap_ref[l] = capacity
            total = total + saturation
        water_ref[s] = total
        low_cond_ref[s] = 0.5 * cond


def sides_kernel(chip_ref, beyond_ref, low_ref, high_ref):
    first = lax.axis_index("core") == 0
    for slot in range(SLOTS):
        chip, beyond = chip_ref[slot], beyond_ref[slot]
        low_ref[slot] = jnp.where(first, beyond, chip)
        high_ref[slot] = jnp.where(first, chip, beyond)


def framed(parts, start, stop):
    def read(l):
        pieces = []
        for at, ref in enumerate(parts):
            lo, hi = max(start - 16 * at, 0), min(stop - 16 * at, 16)
            if lo < hi:
                pieces.append(ref[l, lo:hi, :])
        return jnp.concatenate(pieces, axis=0)

    return read


def step_kernel(step, n_rows_all, *refs):
    first = step == 0
    r0, r1 = SPANS[step]
    rows = r1 - r0
    w0, w1 = WORK[step]
    span = w1 - w0
    work = slice(w0 - r0, w1 - r0)
    own = OWN_ROWS - w0
    refs = list(refs)

    def take(n):
        taken, refs[:n] = refs[:n], []
        return taken

    def take_framed(n):
        low, mid, high = take(n), take(n), take(n)
        return [framed(parts, r0, r1) for parts in zip(low, mid, high)]

    if first:
        head, res, cap, rain, water, low_cond = take_framed(6)
    else:
        (sums_ref,) = take(1)
        old_basis = take(ITERS)
        old_work = slice(r0 - WORK[step - 1][0], r1 - WORK[step - 1][0])
        if step == 1:
            old_head, cond_of, store_of, rain = take_framed(4)
        else:
            (old_head_ref,) = take(1)
            old = slice(r0 - SPANS[step - 1][0], r1 - SPANS[step - 1][0])
            old_head = lambda l: old_head_ref[l, old, :]
            cond_of, store_of, rain = take_framed(3)
        (head_ref,) = take(1)
    v0, v1, v2, v3, inflow_ref, moments_ref = take(6)
    diag_ref, up_ref, dn_ref, ru_ref, rd_ref, xl_ref, xr_ref, flux_ref = take(8)
    if not first:
        res_ref, cap_ref, water_ref, low_cond_ref = take(4)
        head, res, cap, water, low_cond = [
            (lambda l, ref=ref: ref[l]) for ref in (head_ref, res_ref, cap_ref, water_ref, low_cond_ref)
        ]
    basis = (v0, v1, v2, v3)
    section = lax.axis_index("sec")
    band = lax.axis_index("pair") * 2 + lax.axis_index("core")

    if not first:
        change = weights(sums_ref)
        for s in range(SECTIONS):
            total = jnp.zeros((rows, WIDE), F32)
            for q in range(LZ):
                l = s * LZ + q
                h = old_head(l)
                for c, o in zip(change, old_basis):
                    h = h + c * o[l, old_work, :]
                head_ref[l] = h
                saturation, cond, capacity = setup_terms(h, cond_of(l), store_of(l))
                res_ref[l] = recip(cond)
                cap_ref[l] = capacity
                total = total + saturation
            water_ref[s] = total
            low_cond_ref[s] = 0.5 * cond

    flux_ref[0] = rain(step)
    belows = [None] * SECTIONS
    below = None
    for s in reversed(range(SECTIONS)):
        belows[s] = below
        below = water(s) if below is None else below + water(s)
    for s in range(SECTIONS):
        scale = 0.5 if belows[s] is None else 0.5 + 0.5 * belows[s] / (belows[s] + 4.0)
        flux_ref[s + 1] = water(s) * 0.25 * scale * flux_ref[s] + low_cond(s)
        inflow_ref[s] = flux_ref[s, OWN_ROWS - r0 : 2 * OWN_ROWS - r0, 0:OWN_COLS]

    lane = lax.broadcasted_iota(jnp.int32, (span, WIDE), 1)
    col = section * OWN_COLS + lane - jnp.where(lane >= OWN_COLS + HALF, WIDE, 0)
    row = band * OWN_ROWS + (w0 - OWN_ROWS) + lax.broadcasted_iota(jnp.int32, (span, WIDE), 0)
    col_gate = jnp.where((col >= 1) & (col < SECTIONS * OWN_COLS), 2.0, 0.0).astype(F32)
    row_gate = jnp.where((row >= 1) & (row < n_rows_all), 2.0, 0.0).astype(F32)
    kept = slice(own, own + OWN_ROWS)
    none = jnp.zeros((OWN_ROWS, OWN_COLS), F32)

    def faces(l, carry):
        acc, up = carry
        around, tops = res(l), head(l)
        mine, h = around[work], tops[work]
        if l + 1 < NZ:
            dn = 2.0 * recip(mine + res(l + 1)[work])
        else:
            dn = jnp.zeros_like(mine)
        ru = row_gate * recip(mine + turned(around, 1, 0)[work])
        rd = turned(ru, -1, 0)
        xl = col_gate * recip(mine + turned(mine, 1, 1))
        xr = turned(xl, -1, 1)
        diag = cap(l)[work] + up + dn + ru + rd + xl + xr
        inv = recip(diag)
        r = up - dn
        if l % LZ == 0:
            r = r + flux_ref[l // LZ, work, :]
        if l % LZ == LZ - 1:
            r = r - flux_ref[l // LZ + 1, work, :]
        if l > 0:
            r = r + up * (head(l - 1)[work] - h)
        if l + 1 < NZ:
            r = r + dn * (head(l + 1)[work] - h)
        r = r + ru * (turned(tops, 1, 0)[work] - h) + rd * (turned(tops, -1, 0)[work] - h)
        r = r + xl * (turned(h, 1, 1) - h) + xr * (turned(h, -1, 1) - h)
        z = r * inv
        v0[l] = z
        diag_ref[l] = diag[kept, 0:OWN_COLS]
        if l > 0:
            up_ref[l] = up * inv
        if l + 1 < NZ:
            dn_ref[l] = dn * inv
        ru_ref[l] = ru * inv
        rd_ref[l] = rd * inv
        xl_ref[l] = xl * inv
        xr_ref[l] = xr * inv
        return acc + (r * z)[kept, 0:OWN_COLS], dn

    moments = [loop(NZ, faces, (none, jnp.zeros((span, WIDE), F32)))[0]]

    for k in range(1, ITERS):
        src, dst = basis[k - 1], basis[k]

        def smooth(l, accs):
            v = src[l]
            new = ru_ref[l] * turned(v, 1, 0) + rd_ref[l] * turned(v, -1, 0)
            new = new + xl_ref[l] * turned(v, 1, 1) + xr_ref[l] * turned(v, -1, 1)
            if l > 0:
                new = new + up_ref[l] * src[l - 1]
            if l + 1 < NZ:
                new = new + dn_ref[l] * src[l + 1]
            dst[l] = new
            mine = new[kept, 0:OWN_COLS]
            scaled = mine * diag_ref[l]
            return accs[0] + v[kept, 0:OWN_COLS] * scaled, accs[1] + mine * scaled

        moments.extend(loop(NZ, smooth, (none, none)))

    def last(l, acc):
        v = v3[l, own - 8 : own + OWN_ROWS, :]
        mine = v[8:, 0:OWN_COLS]
        pairs = ru_ref[l, kept, 0:OWN_COLS] * turned(v, 1, 0)[8:, 0:OWN_COLS]
        pairs = pairs + xl_ref[l, kept, 0:OWN_COLS] * turned(v, 1, 1)[8:, 0:OWN_COLS]
        if l > 0:
            pairs = pairs + up_ref[l, kept, 0:OWN_COLS] * v3[l - 1, kept, 0:OWN_COLS]
        return acc + 2.0 * mine * diag_ref[l] * pairs

    moments.append(loop(NZ, last, none))

    spot = lax.broadcasted_iota(jnp.int32, (8, 128), 1)
    line = jnp.zeros((8, 128), F32)
    for k, acc in enumerate(moments):
        value = jnp.sum(jnp.sum(acc, axis=0, keepdims=True), axis=1, keepdims=True)
        line = jnp.where(spot == k, value, line)
    moments_ref[...] = line


def last_kernel(sums_ref, head_ref, v0, v1, v2, v3, i0, i1, i2, out_ref):
    change = weights(sums_ref)
    own = OWN_ROWS - WORK[2][0]
    kept = slice(own, own + OWN_ROWS)
    for l in range(NZ):
        h = head_ref[l, OWN_ROWS - SPANS[2][0] : 2 * OWN_ROWS - SPANS[2][0], 0:OWN_COLS]
        for c, o in zip(change, (v0, v1, v2, v3)):
            h = h + c * o[l, kept, 0:OWN_COLS]
        out_ref[l // LZ, l % LZ] = h
    for s in range(SECTIONS):
        for c, i in enumerate((i0, i1, i2)):
            out_ref[s, LZ + c] = i[s]


def shape(*dims):
    return jax.ShapeDtypeStruct(dims, F32)


def near(*dims):
    return pltpu.VMEM(dims, F32)


def held(*arrays, space=pltpu.VMEM):
    return tuple(pltpu.with_memory_space_constraint(x, space) for x in arrays)


def call(kernel, operands, outs, scratch=(), in_specs=None, out_specs=None, **more):
    return pl.pallas_call(
        kernel,
        **more,
        out_shape=outs,
        in_specs=in_specs or [VMEM] * len(operands),
        out_specs=out_specs or jax.tree.map(lambda _: VMEM, outs),
        scratch_shapes=[pltpu.VMEM(dims, F32) if isinstance(dims, tuple) else dims for dims in scratch],
        compiler_params=params(),
    )(*operands)


def join_kernel(parts_ref, head_hbm, flows_hbm, sems):
    copies = []
    for t in range(SECTIONS):
        cols = slice(t * OWN_COLS, (t + 1) * OWN_COLS)
        copies.append(pltpu.make_async_copy(parts_ref.at[t, 0:LZ], head_hbm.at[:, :, cols], sems.at[0, t]))
        copies.append(pltpu.make_async_copy(parts_ref.at[t, LZ : LZ + 3], flows_hbm.at[0, :, :, cols], sems.at[1, t]))
    for copy in copies:
        copy.start()
    for copy in copies:
        copy.wait()


def add_up(moments):
    chips = SECTIONS * lax.axis_size("pair")
    both = moments + lax.ppermute(moments, "core", [(0, 1), (1, 0)])
    rows = lax.all_to_all(jnp.broadcast_to(both[:1, None], (chips, 1, 128)), ("sec", "pair"), 0, 0, tiled=True)
    return rows.reshape(chips, 128)


def body(pressure_start, soil_type, saturated_conductivity, storage_coefficient, rainfall):
    gx = ("pair", "core")
    bands = 2 * lax.axis_size("pair")
    outside = pl.BlockSpec(memory_space=pl.ANY)
    block = (LZ, OWN_ROWS, SECTIONS * OWN_COLS)
    packed = call(
        split_kernel,
        held(pressure_start, soil_type, space=pltpu.HBM),
        near(SECTIONS, 9, OWN_ROWS, OWN_COLS),
        (block, pltpu.VMEM(block, jnp.int32), pltpu.SemaphoreType.DMA((2,))),
        in_specs=[outside] * 2,
    )
    mid = lax.all_to_all(packed, "sec", 0, 0, tiled=True)
    to_send = call(edges_kernel, held(mid, rainfall), near(SLOTS, OWN_ROWS, OWN_COLS))
    pairs = [(i, i + 1) for i in range(1, bands - 1, 2)]
    beyond = lax.ppermute(to_send, gx, pairs + [(j, i) for i, j in pairs])
    chip = lax.ppermute(to_send, "core", [(0, 1), (1, 0)])
    low, high = call(sides_kernel, held(chip, beyond), [near(SLOTS, OWN_ROWS, OWN_COLS)] * 2)
    tables = jnp.stack([saturated_conductivity, storage_coefficient])
    tables = jnp.broadcast_to(jnp.pad(tables, ((0, 0), (0, 128 - tables.shape[1])))[:, None, :], (2, 8, 128))

    def entered(rows_sent):
        return call(
            enter_kernel,
            (*held(rows_sent), tables),
            [near(n, OWN_ROWS, WIDE) for n in (NZ,) * 5 + (3,) + (SECTIONS,) * 2],
            cost_estimate=pl.CostEstimate(flops=10_000_000, bytes_accessed=4_000_000, transcendentals=300_000),
        )

    parts = [entered(low), entered(to_send), entered(high)]

    def pick(*which):
        return [part[k] for part in parts for k in which]

    inflows = []
    state = None
    for step, (r0, r1) in enumerate(SPANS):
        rows = r1 - r0
        field = (NZ, rows, WIDE)
        basis = (NZ, WORK[step][1] - WORK[step][0], WIDE)
        outs = [near(*field)] + [near(*basis)] * 4
        kernel = functools.partial(step_kernel, step, bands * OWN_ROWS)
        tail = [near(SECTIONS, OWN_ROWS, OWN_COLS), near(8, 128)]
        scratch = [(NZ, OWN_ROWS, OWN_COLS)] + [basis] * 6 + [(SECTIONS + 1, rows, WIDE)]
        if step == 0:
            got = call(kernel, held(*pick(0, 3, 4, 5, 6, 7)), [near(*basis)] * 4 + tail, scratch)
            v = got[:4]
        else:
            state = pick(0, 1, 2, 5) if step == 1 else [head, *pick(1, 2, 5)]
            soil = [field] * 2 + [(SECTIONS, rows, WIDE)] * 2
            got = call(kernel, (sums, *held(*v, *state)), outs + tail, scratch + soil)
            head, v = got[0], got[1:5]
        inflows.append(got[-2])
        sums = add_up(got[-1])
    out = call(last_kernel, (sums, *held(head, *v, *inflows)), near(SECTIONS, 7, OWN_ROWS, OWN_COLS))
    out = lax.all_to_all(out, "sec", 0, 0, tiled=True)
    return call(
        join_kernel,
        held(out),
        [shape(*block), shape(1, 3, *block[1:])],
        (pltpu.SemaphoreType.DMA((2, SECTIONS)),),
        out_specs=[outside] * 2,
    )


def solution(mesh):
    sections, bands = mesh.devices.shape
    gx = ("pair", "core")
    placed = (P("sec", gx, None), P("sec", gx, None), P(), P(), P(None, gx, None))
    return jax.shard_map(
        body,
        mesh=jax.sharding.Mesh(mesh.devices.reshape(sections, bands // 2, 2), ("sec", *gx)),
        in_specs=placed,
        out_specs=(P("sec", gx, None), P("sec", None, gx, None)),
        check_vma=False,
    )
```

```python
import functools

import jax
import jax.numpy as jnp
from jax import lax
from jax.experimental import pallas as pl
from jax.experimental.pallas import tpu as pltpu
from jax.sharding import PartitionSpec as P

ITERS = 4
SECTIONS = 4
LZ = 4
NZ = SECTIONS * LZ
OWN_ROWS = 16
OWN_COLS = 256
WIDE = 384
HALF = 64
EDGE = 16
FRAME = 48
SLOTS = 40
REACH = 13
SPANS = ((0, 48), (0, 40), (8, 40))
WORK = ((0, 48), (8, 40), (8, 40))
F32 = jnp.float32
VMEM = pl.BlockSpec(memory_space=pltpu.VMEM)


def params():
    return pltpu.CompilerParams(vmem_limit_bytes=24 * 1024 * 1024)


def turned(x, by, axis):
    return pltpu.roll(x, by % x.shape[axis], axis)


def lanes(rows):
    return lax.broadcasted_iota(jnp.int32, (rows, 128), 1)


def tail_of(after, before):
    return jnp.where(lanes(after.shape[0]) < EDGE, after, turned(before, 2 * EDGE, 1))


def grouped(tails):
    lane = lanes(tails[0].shape[0])
    tile = tails[0]
    for j in range(1, len(tails)):
        tile = jnp.where(lane >= 2 * EDGE * j, turned(tails[j], 2 * EDGE * j, 1), tile)
    return tile


def spread(tile, count):
    for _ in range(count):
        later = turned(tile, -2 * EDGE, 1)
        yield jnp.where(lanes(tile.shape[0]) < HALF, tile, later)
        tile = later


def split_kernel(head_hbm, soil_hbm, out_ref, head_ref, soil_ref, sems):
    copies = [
        pltpu.make_async_copy(head_hbm, head_ref, sems.at[0]),
        pltpu.make_async_copy(soil_hbm, soil_ref, sems.at[1]),
    ]
    for copy in copies:
        copy.start()
    whole = SECTIONS * OWN_COLS
    for part, ref in enumerate((head_ref, soil_ref)):
        copies[part].wait()
        for target in range(SECTIONS):
            start = target * OWN_COLS
            after, before = (start + OWN_COLS) % whole, (start - 128) % whole
            tails = []
            for q in range(LZ):
                field = ref[q].astype(F32)
                out_ref[target, part * LZ + q] = field[:, start : start + OWN_COLS]
                tails.append(tail_of(field[:, after : after + 128], field[:, before : before + 128]))
            out_ref[target, 2 * LZ, :, 128 * part : 128 * part + 128] = grouped(tails)


def edges_kernel(mid_ref, rain_ref, out_ref, beyond_ref):
    section = lax.axis_index("sec")
    start = pl.multiple_of(section * OWN_COLS, OWN_COLS)
    after = pl.multiple_of(lax.rem(section + 1, SECTIONS) * OWN_COLS, OWN_COLS)
    before = pl.multiple_of(lax.rem(section + SECTIONS - 1, SECTIONS) * OWN_COLS + 128, 128)
    tails = []
    for c in range(3):
        out_ref[36 + c] = rain_ref[c, :, pl.ds(start, OWN_COLS)]
        tails.append(tail_of(rain_ref[c, :, pl.ds(after, 128)], rain_ref[c, :, pl.ds(before, 128)]))
    out_ref[39] = jnp.concatenate([grouped(tails), jnp.zeros((OWN_ROWS, 128), F32)], axis=1)
    for slot in range(36):
        out_ref[slot] = mid_ref[slot // 9, slot % 9]
    first = lax.axis_index("core") == 0
    for slot in range(SLOTS):
        field = out_ref[slot]
        beyond_ref[REACH * slot : REACH * slot + REACH, :] = jnp.where(first, field[:REACH], field[OWN_ROWS - REACH :])


def weights(sums_ref):
    total = jnp.sum(sums_ref[...], axis=0, keepdims=True)
    lane = lax.broadcasted_iota(jnp.int32, total.shape, 1)
    m = [jnp.sum(jnp.where(lane == k, total, 0.0), axis=1, keepdims=True) for k in range(8)]
    step_m = [m[k] - m[k + 1] for k in range(7)]
    zero = jnp.zeros_like(m[0])

    def form(poly, other, table):
        result = zero
        for i, a in enumerate(poly):
            for j, b in enumerate(other):
                result = result + a * b * table[i + j]
        return result

    z = [jnp.ones_like(zero)]
    direction = z
    rz = m[0]
    change = [zero] * ITERS
    for turn in range(ITERS):
        below = form(direction, direction, step_m)
        alpha = jnp.where(below > 0.0, rz / jnp.where(below > 0.0, below, 1.0), 0.0)
        for i, a in enumerate(direction):
            change[i] = change[i] + alpha * a
        if turn + 1 < ITERS:
            long = direction + [zero]
            image = [long[i] - (long[i - 1] if i else zero) for i in range(len(long))]
            z = [a - alpha * b for a, b in zip(z + [zero], image)]
            renewed = form(z, z, m)
            beta = jnp.where(rz > 0.0, renewed / jnp.where(rz > 0.0, rz, 1.0), 0.0)
            direction = [a + beta * b for a, b in zip(z, long)]
            rz = renewed
    return change


def loop(n, f, init):
    for i in range(n):
        init = f(i, init)
    return init


def recip(x):
    return pl.reciprocal(x, approx=False)


def setup_terms(h, cond_table, store_table):
    saturation = recip(1.0 + jnp.exp(-h))
    cond = cond_table * (0.05 + saturation * saturation)
    capacity = store_table * (0.1 + saturation * (1.0 - saturation))
    return saturation, cond, capacity


def gather(table, kinds):
    rows, cols = kinds.shape
    parts = []
    for j in range(cols // 128):
        parts.append(
            jnp.concatenate(
                [
                    jnp.take_along_axis(table, kinds[8 * i : 8 * i + 8, 128 * j : 128 * j + 128], axis=1, mode="promise_in_bounds")
                    for i in range(rows // 8)
                ],
                axis=0,
            )
        )
    return jnp.concatenate(parts, axis=1)


def enter_kernel(from_ref, tables_ref, head_ref, cond_ref, store_ref, res_ref, cap_ref, rain_ref, water_ref, low_cond_ref):
    packs = [(rain_ref, 0, 36, 39, 0, 3)]
    for s in range(SECTIONS):
        packs.append((head_ref, s * LZ, 9 * s, 9 * s + 8, 0, LZ))
        packs.append((cond_ref, s * LZ, 9 * s + LZ, 9 * s + 8, 1, LZ))
    for ref, first, slot, halo, tile, count in packs:
        for q, third in enumerate(spread(from_ref[halo, :, 128 * tile : 128 * tile + 128], count)):
            ref[first + q, :, 0:OWN_COLS] = from_ref[slot + q]
            ref[first + q, :, OWN_COLS:WIDE] = third
    for l in range(NZ):
        store_ref[l] = gather(tables_ref[1], cond_ref[l].astype(jnp.int32))
    for l in range(NZ):
        cond_ref[l] = gather(tables_ref[0], cond_ref[l].astype(jnp.int32))
    for s in range(SECTIONS):
        total = jnp.zeros((OWN_ROWS, WIDE), F32)
        for q in range(LZ):
            l = s * LZ + q
            saturation, cond, capacity = setup_terms(head_ref[l], cond_ref[l], store_ref[l])
            res_ref[l] = recip(cond)
            cap_ref[l] = capacity
            total = total + saturation
        water_ref[s] = total
        low_cond_ref[s] = 0.5 * cond


def sides_kernel(chip_ref, beyond_ref, low_ref, high_ref):
    first = lax.axis_index("core") == 0
    for slot in range(SLOTS):
        chip, beyond = chip_ref[slot], beyond_ref[REACH * slot : REACH * slot + REACH, :]
        gap = jnp.zeros((OWN_ROWS - REACH, OWN_COLS), F32)
        beyond = jnp.where(first, jnp.concatenate([gap, beyond], axis=0), jnp.concatenate([beyond, gap], axis=0))
        low_ref[slot] = jnp.where(first, beyond, chip)
        high_ref[slot] = jnp.where(first, chip, beyond)


def framed(parts, start, stop):
    def read(l):
        pieces = []
        for at, ref in enumerate(parts):
            lo, hi = max(start - 16 * at, 0), min(stop - 16 * at, 16)
            if lo < hi:
                pieces.append(ref[l, lo:hi, :])
        return jnp.concatenate(pieces, axis=0)

    return read


def step_kernel(step, n_rows_all, *refs):
    first = step == 0
    r0, r1 = SPANS[step]
    rows = r1 - r0
    w0, w1 = WORK[step]
    span = w1 - w0
    work = slice(w0 - r0, w1 - r0)
    own = OWN_ROWS - w0
    refs = list(refs)

    def take(n):
        taken, refs[:n] = refs[:n], []
        return taken

    def take_framed(n):
        low, mid, high = take(n), take(n), take(n)
        return [framed(parts, r0, r1) for parts in zip(low, mid, high)]

    if first:
        head, res, cap, rain, water, low_cond = take_framed(6)
    else:
        (sums_ref,) = take(1)
        old_basis = take(ITERS)
        old_work = slice(r0 - WORK[step - 1][0], r1 - WORK[step - 1][0])
        if step == 1:
            old_head, cond_of, store_of, rain = take_framed(4)
        else:
            (old_head_ref,) = take(1)
            old = slice(r0 - SPANS[step - 1][0], r1 - SPANS[step - 1][0])
            old_head = lambda l: old_head_ref[l, old, :]
            cond_of, store_of, rain = take_framed(3)
        (head_ref,) = take(1)
    v0, v1, v2, v3, inflow_ref, moments_ref = take(6)
    diag_ref, up_ref, dn_ref, ru_ref, rd_ref, xl_ref, xr_ref, flux_ref = take(8)
    if not first:
        res_ref, cap_ref, water_ref, low_cond_ref = take(4)
        head, res, cap, water, low_cond = [
            (lambda l, ref=ref: ref[l]) for ref in (head_ref, res_ref, cap_ref, water_ref, low_cond_ref)
        ]
    basis = (v0, v1, v2, v3)
    section = lax.axis_index("sec")
    band = lax.axis_index("pair") * 2 + lax.axis_index("core")

    if not first:
        change = weights(sums_ref)
        for s in range(SECTIONS):
            total = jnp.zeros((rows, WIDE), F32)
            for q in range(LZ):
                l = s * LZ + q
                h = old_head(l)
                for c, o in zip(change, old_basis):
                    h = h + c * o[l, old_work, :]
                head_ref[l] = h
                saturation, cond, capacity = setup_terms(h, cond_of(l), store_of(l))
                res_ref[l] = recip(cond)
                cap_ref[l] = capacity
                total = total + saturation
            water_ref[s] = total
            low_cond_ref[s] = 0.5 * cond

    flux_ref[0] = rain(step)
    belows = [None] * SECTIONS
    below = None
    for s in reversed(range(SECTIONS)):
        belows[s] = below
        below = water(s) if below is None else below + water(s)
    for s in range(SECTIONS):
        scale = 0.5 if belows[s] is None else 0.5 + 0.5 * belows[s] / (belows[s] + 4.0)
        flux_ref[s + 1] = water(s) * 0.25 * scale * flux_ref[s] + low_cond(s)
        inflow_ref[s] = flux_ref[s, OWN_ROWS - r0 : 2 * OWN_ROWS - r0, 0:OWN_COLS]

    lane = lax.broadcasted_iota(jnp.int32, (span, WIDE), 1)
    col = section * OWN_COLS + lane - jnp.where(lane >= OWN_COLS + HALF, WIDE, 0)
    row = band * OWN_ROWS + (w0 - OWN_ROWS) + lax.broadcasted_iota(jnp.int32, (span, WIDE), 0)
    col_gate = jnp.where((col >= 1) & (col < SECTIONS * OWN_COLS), 2.0, 0.0).astype(F32)
    row_gate = jnp.where((row >= 1) & (row < n_rows_all), 2.0, 0.0).astype(F32)
    kept = slice(own, own + OWN_ROWS)
    none = jnp.zeros((OWN_ROWS, OWN_COLS), F32)

    def faces(l, carry):
        acc, up = carry
        around, tops = res(l), head(l)
        mine, h = around[work], tops[work]
        if l + 1 < NZ:
            dn = 2.0 * recip(mine + res(l + 1)[work])
        else:
            dn = jnp.zeros_like(mine)
        ru = row_gate * recip(mine + turned(around, 1, 0)[work])
        rd = turned(ru, -1, 0)
        xl = col_gate * recip(mine + turned(mine, 1, 1))
        xr = turned(xl, -1, 1)
        diag = cap(l)[work] + up + dn + ru + rd + xl + xr
        inv = recip(diag)
        r = up - dn
        if l % LZ == 0:
            r = r + flux_ref[l // LZ, work, :]
        if l % LZ == LZ - 1:
            r = r - flux_ref[l // LZ + 1, work, :]
        if l > 0:
            r = r + up * (head(l - 1)[work] - h)
        if l + 1 < NZ:
            r = r + dn * (head(l + 1)[work] - h)
        r = r + ru * (turned(tops, 1, 0)[work] - h) + rd * (turned(tops, -1, 0)[work] - h)
        r = r + xl * (turned(h, 1, 1) - h) + xr * (turned(h, -1, 1) - h)
        z = r * inv
        v0[l] = z
        diag_ref[l] = diag[kept, 0:OWN_COLS]
        if l > 0:
            up_ref[l] = up * inv
        if l + 1 < NZ:
            dn_ref[l] = dn * inv
        ru_ref[l] = ru * inv
        rd_ref[l] = rd * inv
        xl_ref[l] = xl * inv
        xr_ref[l] = xr * inv
        return acc + (r * z)[kept, 0:OWN_COLS], dn

    moments = [loop(NZ, faces, (none, jnp.zeros((span, WIDE), F32)))[0]]

    for k in range(1, ITERS):
        src, dst = basis[k - 1], basis[k]

        def smooth(l, accs):
            v = src[l]
            new = ru_ref[l] * turned(v, 1, 0) + rd_ref[l] * turned(v, -1, 0)
            new = new + xl_ref[l] * turned(v, 1, 1) + xr_ref[l] * turned(v, -1, 1)
            if l > 0:
                new = new + up_ref[l] * src[l - 1]
            if l + 1 < NZ:
                new = new + dn_ref[l] * src[l + 1]
            dst[l] = new
            mine = new[kept, 0:OWN_COLS]
            scaled = mine * diag_ref[l]
            return accs[0] + v[kept, 0:OWN_COLS] * scaled, accs[1] + mine * scaled

        moments.extend(loop(NZ, smooth, (none, none)))

    def last(l, acc):
        v = v3[l, own - 8 : own + OWN_ROWS, :]
        mine = v[8:, 0:OWN_COLS]
        pairs = ru_ref[l, kept, 0:OWN_COLS] * turned(v, 1, 0)[8:, 0:OWN_COLS]
        pairs = pairs + xl_ref[l, kept, 0:OWN_COLS] * turned(v, 1, 1)[8:, 0:OWN_COLS]
        if l > 0:
            pairs = pairs + up_ref[l, kept, 0:OWN_COLS] * v3[l - 1, kept, 0:OWN_COLS]
        return acc + 2.0 * mine * diag_ref[l] * pairs

    moments.append(loop(NZ, last, none))

    spot = lax.broadcasted_iota(jnp.int32, (8, 128), 1)
    line = jnp.zeros((8, 128), F32)
    for k, acc in enumerate(moments):
        value = jnp.sum(jnp.sum(acc, axis=0, keepdims=True), axis=1, keepdims=True)
        line = jnp.where(spot == k, value, line)
    moments_ref[...] = line


def last_kernel(sums_ref, head_ref, v0, v1, v2, v3, i0, i1, i2, out_ref):
    change = weights(sums_ref)
    own = OWN_ROWS - WORK[2][0]
    kept = slice(own, own + OWN_ROWS)
    for l in range(NZ):
        h = head_ref[l, OWN_ROWS - SPANS[2][0] : 2 * OWN_ROWS - SPANS[2][0], 0:OWN_COLS]
        for c, o in zip(change, (v0, v1, v2, v3)):
            h = h + c * o[l, kept, 0:OWN_COLS]
        out_ref[l // LZ, l % LZ] = h
    for s in range(SECTIONS):
        for c, i in enumerate((i0, i1, i2)):
            out_ref[s, LZ + c] = i[s]


def shape(*dims):
    return jax.ShapeDtypeStruct(dims, F32)


def near(*dims):
    return pltpu.VMEM(dims, F32)


def held(*arrays, space=pltpu.VMEM):
    return tuple(pltpu.with_memory_space_constraint(x, space) for x in arrays)


def call(kernel, operands, outs, scratch=(), in_specs=None, out_specs=None, **more):
    return pl.pallas_call(
        kernel,
        **more,
        out_shape=outs,
        in_specs=in_specs or [VMEM] * len(operands),
        out_specs=out_specs or jax.tree.map(lambda _: VMEM, outs),
        scratch_shapes=[pltpu.VMEM(dims, F32) if isinstance(dims, tuple) else dims for dims in scratch],
        compiler_params=params(),
    )(*operands)


def join_kernel(parts_ref, head_hbm, flows_hbm, sems):
    copies = []
    for t in range(SECTIONS):
        cols = slice(t * OWN_COLS, (t + 1) * OWN_COLS)
        copies.append(pltpu.make_async_copy(parts_ref.at[t, 0:LZ], head_hbm.at[:, :, cols], sems.at[0, t]))
        copies.append(pltpu.make_async_copy(parts_ref.at[t, LZ : LZ + 3], flows_hbm.at[0, :, :, cols], sems.at[1, t]))
    for copy in copies:
        copy.start()
    for copy in copies:
        copy.wait()


def add_up(moments):
    chips = SECTIONS * lax.axis_size("pair")
    both = moments + lax.ppermute(moments, "core", [(0, 1), (1, 0)])
    rows = lax.all_to_all(jnp.broadcast_to(both[:1, None], (chips, 1, 128)), ("sec", "pair"), 0, 0, tiled=True)
    return rows.reshape(chips, 128)


def body(pressure_start, soil_type, saturated_conductivity, storage_coefficient, rainfall):
    gx = ("pair", "core")
    bands = 2 * lax.axis_size("pair")
    outside = pl.BlockSpec(memory_space=pl.ANY)
    block = (LZ, OWN_ROWS, SECTIONS * OWN_COLS)
    packed = call(
        split_kernel,
        held(pressure_start, soil_type, space=pltpu.HBM),
        near(SECTIONS, 9, OWN_ROWS, OWN_COLS),
        (block, pltpu.VMEM(block, jnp.int32), pltpu.SemaphoreType.DMA((2,))),
        in_specs=[outside] * 2,
    )
    mid = lax.all_to_all(packed, "sec", 0, 0, tiled=True)
    to_send, to_beyond = call(
        edges_kernel, held(mid, rainfall), [near(SLOTS, OWN_ROWS, OWN_COLS), near(REACH * SLOTS, OWN_COLS)]
    )
    pairs = [(i, i + 1) for i in range(1, bands - 1, 2)]
    beyond = lax.ppermute(to_beyond, gx, pairs + [(j, i) for i, j in pairs])
    chip = lax.ppermute(to_send, "core", [(0, 1), (1, 0)])
    low, high = call(sides_kernel, held(chip, beyond), [near(SLOTS, OWN_ROWS, OWN_COLS)] * 2)
    tables = jnp.stack([saturated_conductivity, storage_coefficient])
    tables = jnp.broadcast_to(jnp.pad(tables, ((0, 0), (0, 128 - tables.shape[1])))[:, None, :], (2, 8, 128))

    def entered(rows_sent):
        return call(
            enter_kernel,
            (*held(rows_sent), tables),
            [near(n, OWN_ROWS, WIDE) for n in (NZ,) * 5 + (3,) + (SECTIONS,) * 2],
            cost_estimate=pl.CostEstimate(flops=10_000_000, bytes_accessed=4_000_000, transcendentals=300_000),
        )

    parts = [entered(low), entered(to_send), entered(high)]

    def pick(*which):
        return [part[k] for part in parts for k in which]

    inflows = []
    state = None
    for step, (r0, r1) in enumerate(SPANS):
        rows = r1 - r0
        field = (NZ, rows, WIDE)
        basis = (NZ, WORK[step][1] - WORK[step][0], WIDE)
        outs = [near(*field)] + [near(*basis)] * 4
        kernel = functools.partial(step_kernel, step, bands * OWN_ROWS)
        tail = [near(SECTIONS, OWN_ROWS, OWN_COLS), near(8, 128)]
        scratch = [(NZ, OWN_ROWS, OWN_COLS)] + [basis] * 6 + [(SECTIONS + 1, rows, WIDE)]
        if step == 0:
            got = call(kernel, held(*pick(0, 3, 4, 5, 6, 7)), [near(*basis)] * 4 + tail, scratch)
            v = got[:4]
        else:
            state = pick(0, 1, 2, 5) if step == 1 else [head, *pick(1, 2, 5)]
            soil = [field] * 2 + [(SECTIONS, rows, WIDE)] * 2
            got = call(kernel, (sums, *held(*v, *state)), outs + tail, scratch + soil)
            head, v = got[0], got[1:5]
        inflows.append(got[-2])
        sums = add_up(got[-1])
    out = call(last_kernel, (sums, *held(head, *v, *inflows)), near(SECTIONS, 7, OWN_ROWS, OWN_COLS))
    out = lax.all_to_all(out, "sec", 0, 0, tiled=True)
    return call(
        join_kernel,
        held(out),
        [shape(*block), shape(1, 3, *block[1:])],
        (pltpu.SemaphoreType.DMA((2, SECTIONS)),),
        out_specs=[outside] * 2,
    )


def solution(mesh):
    sections, bands = mesh.devices.shape
    gx = ("pair", "core")
    placed = (P("sec", gx, None), P("sec", gx, None), P(), P(), P(None, gx, None))
    return jax.shard_map(
        body,
        mesh=jax.sharding.Mesh(mesh.devices.reshape(sections, bands // 2, 2), ("sec", *gx)),
        in_specs=placed,
        out_specs=(P("sec", gx, None), P("sec", None, gx, None)),
        check_vma=False,
    )
```

```python
import functools

import jax
import jax.numpy as jnp
from jax import lax
from jax.experimental import pallas as pl
from jax.experimental.pallas import tpu as pltpu
from jax.sharding import PartitionSpec as P

ITERS = 4
SECTIONS = 4
LZ = 4
NZ = SECTIONS * LZ
OWN_ROWS = 16
OWN_COLS = 256
WIDE = 384
HALF = 64
EDGE = 16
FRAME = 48
SLOTS = 40
REACH = 13
SPANS = ((0, 48), (0, 40), (8, 40))
WORK = ((0, 48), (8, 40), (8, 40))
F32 = jnp.float32
VMEM = pl.BlockSpec(memory_space=pltpu.VMEM)


def params():
    return pltpu.CompilerParams(vmem_limit_bytes=24 * 1024 * 1024)


def turned(x, by, axis):
    return pltpu.roll(x, by % x.shape[axis], axis)


def lanes(rows):
    return lax.broadcasted_iota(jnp.int32, (rows, 128), 1)


def tail_of(after, before):
    return jnp.where(lanes(after.shape[0]) < EDGE, after, turned(before, 2 * EDGE, 1))


def grouped(tails):
    lane = lanes(tails[0].shape[0])
    tile = tails[0]
    for j in range(1, len(tails)):
        tile = jnp.where(lane >= 2 * EDGE * j, turned(tails[j], 2 * EDGE * j, 1), tile)
    return tile


def spread(tile, count):
    for _ in range(count):
        later = turned(tile, -2 * EDGE, 1)
        yield jnp.where(lanes(tile.shape[0]) < HALF, tile, later)
        tile = later


def split_kernel(head_hbm, soil_hbm, out_ref, head_ref, soil_ref, sems):
    copies = [
        pltpu.make_async_copy(head_hbm, head_ref, sems.at[0]),
        pltpu.make_async_copy(soil_hbm, soil_ref, sems.at[1]),
    ]
    for copy in copies:
        copy.start()
    whole = SECTIONS * OWN_COLS
    for part, ref in enumerate((head_ref, soil_ref)):
        copies[part].wait()
        for target in range(SECTIONS):
            start = target * OWN_COLS
            after, before = (start + OWN_COLS) % whole, (start - 128) % whole
            tails = []
            for q in range(LZ):
                field = ref[q].astype(F32)
                out_ref[target, part * LZ + q] = field[:, start : start + OWN_COLS]
                tails.append(tail_of(field[:, after : after + 128], field[:, before : before + 128]))
            out_ref[target, 2 * LZ, :, 128 * part : 128 * part + 128] = grouped(tails)


def edges_kernel(mid_ref, rain_ref, beyond_ref, chip_ref, rain_out_ref):
    section = lax.axis_index("sec")
    start = pl.multiple_of(section * OWN_COLS, OWN_COLS)
    after = pl.multiple_of(lax.rem(section + 1, SECTIONS) * OWN_COLS, OWN_COLS)
    before = pl.multiple_of(lax.rem(section + SECTIONS - 1, SECTIONS) * OWN_COLS + 128, 128)
    tails = []
    for c in range(3):
        rain_out_ref[c] = rain_ref[c, :, pl.ds(start, OWN_COLS)]
        tails.append(tail_of(rain_ref[c, :, pl.ds(after, 128)], rain_ref[c, :, pl.ds(before, 128)]))
    rain_out_ref[3] = jnp.concatenate([grouped(tails), jnp.zeros((OWN_ROWS, 128), F32)], axis=1)
    first = lax.axis_index("core") == 0
    beyond_ref[REACH * SLOTS :, :] = jnp.zeros((8, OWN_COLS), F32)
    for slot in range(SLOTS):
        field = mid_ref[slot // 9, slot % 9] if slot < 36 else rain_out_ref[slot - 36]
        at = slice(REACH * slot, REACH * slot + REACH)
        top, bottom = field[:REACH], field[OWN_ROWS - REACH :]
        beyond_ref[at, :] = jnp.where(first, top, bottom)
        chip_ref[at, :] = jnp.where(first, bottom, top)


def whole_kernel(mid_ref, rain_ref, out_ref):
    for slot in range(SLOTS):
        out_ref[slot] = mid_ref[slot // 9, slot % 9] if slot < 36 else rain_ref[slot - 36]


def weights(sums_ref):
    total = jnp.sum(sums_ref[...], axis=0, keepdims=True)
    lane = lax.broadcasted_iota(jnp.int32, total.shape, 1)
    m = [jnp.sum(jnp.where(lane == k, total, 0.0), axis=1, keepdims=True) for k in range(8)]
    step_m = [m[k] - m[k + 1] for k in range(7)]
    zero = jnp.zeros_like(m[0])

    def form(poly, other, table):
        result = zero
        for i, a in enumerate(poly):
            for j, b in enumerate(other):
                result = result + a * b * table[i + j]
        return result

    z = [jnp.ones_like(zero)]
    direction = z
    rz = m[0]
    change = [zero] * ITERS
    for turn in range(ITERS):
        below = form(direction, direction, step_m)
        alpha = jnp.where(below > 0.0, rz / jnp.where(below > 0.0, below, 1.0), 0.0)
        for i, a in enumerate(direction):
            change[i] = change[i] + alpha * a
        if turn + 1 < ITERS:
            long = direction + [zero]
            image = [long[i] - (long[i - 1] if i else zero) for i in range(len(long))]
            z = [a - alpha * b for a, b in zip(z + [zero], image)]
            renewed = form(z, z, m)
            beta = jnp.where(rz > 0.0, renewed / jnp.where(rz > 0.0, rz, 1.0), 0.0)
            direction = [a + beta * b for a, b in zip(z, long)]
            rz = renewed
    return change


def loop(n, f, init):
    for i in range(n):
        init = f(i, init)
    return init


def recip(x):
    return pl.reciprocal(x, approx=False)


def setup_terms(h, cond_table, store_table):
    saturation = recip(1.0 + jnp.exp(-h))
    cond = cond_table * (0.05 + saturation * saturation)
    capacity = store_table * (0.1 + saturation * (1.0 - saturation))
    return saturation, cond, capacity


def gather(table, kinds):
    rows, cols = kinds.shape
    parts = []
    for j in range(cols // 128):
        parts.append(
            jnp.concatenate(
                [
                    jnp.take_along_axis(table, kinds[8 * i : 8 * i + 8, 128 * j : 128 * j + 128], axis=1, mode="promise_in_bounds")
                    for i in range(rows // 8)
                ],
                axis=0,
            )
        )
    return jnp.concatenate(parts, axis=1)


def enter_kernel(from_ref, tables_ref, head_ref, cond_ref, store_ref, res_ref, cap_ref, rain_ref, water_ref, low_cond_ref):
    packs = [(rain_ref, 0, 36, 39, 0, 3)]
    for s in range(SECTIONS):
        packs.append((head_ref, s * LZ, 9 * s, 9 * s + 8, 0, LZ))
        packs.append((cond_ref, s * LZ, 9 * s + LZ, 9 * s + 8, 1, LZ))
    for ref, first, slot, halo, tile, count in packs:
        for q, third in enumerate(spread(from_ref[halo, :, 128 * tile : 128 * tile + 128], count)):
            ref[first + q, :, 0:OWN_COLS] = from_ref[slot + q]
            ref[first + q, :, OWN_COLS:WIDE] = third
    for l in range(NZ):
        store_ref[l] = gather(tables_ref[1], cond_ref[l].astype(jnp.int32))
    for l in range(NZ):
        cond_ref[l] = gather(tables_ref[0], cond_ref[l].astype(jnp.int32))
    for s in range(SECTIONS):
        total = jnp.zeros((OWN_ROWS, WIDE), F32)
        for q in range(LZ):
            l = s * LZ + q
            saturation, cond, capacity = setup_terms(head_ref[l], cond_ref[l], store_ref[l])
            res_ref[l] = recip(cond)
            cap_ref[l] = capacity
            total = total + saturation
        water_ref[s] = total
        low_cond_ref[s] = 0.5 * cond


def sides_kernel(chip_ref, beyond_ref, low_ref, high_ref):
    first = lax.axis_index("core") == 0
    for slot in range(SLOTS):
        at = slice(REACH * slot, REACH * slot + REACH)
        chip, beyond = chip_ref[at, :], beyond_ref[at, :]
        gap = jnp.zeros((OWN_ROWS - REACH, OWN_COLS), F32)
        low_ref[slot] = jnp.concatenate([gap, jnp.where(first, beyond, chip)], axis=0)
        high_ref[slot] = jnp.concatenate([jnp.where(first, chip, beyond), gap], axis=0)


def framed(parts, start, stop):
    def read(l):
        pieces = []
        for at, ref in enumerate(parts):
            lo, hi = max(start - 16 * at, 0), min(stop - 16 * at, 16)
            if lo < hi:
                pieces.append(ref[l, lo:hi, :])
        return jnp.concatenate(pieces, axis=0)

    return read


def step_kernel(step, n_rows_all, *refs):
    first = step == 0
    r0, r1 = SPANS[step]
    rows = r1 - r0
    w0, w1 = WORK[step]
    span = w1 - w0
    work = slice(w0 - r0, w1 - r0)
    own = OWN_ROWS - w0
    refs = list(refs)

    def take(n):
        taken, refs[:n] = refs[:n], []
        return taken

    def take_framed(n):
        low, mid, high = take(n), take(n), take(n)
        return [framed(parts, r0, r1) for parts in zip(low, mid, high)]

    if first:
        head, res, cap, rain, water, low_cond = take_framed(6)
    else:
        (sums_ref,) = take(1)
        old_basis = take(ITERS)
        old_work = slice(r0 - WORK[step - 1][0], r1 - WORK[step - 1][0])
        if step == 1:
            old_head, cond_of, store_of, rain = take_framed(4)
        else:
            (old_head_ref,) = take(1)
            old = slice(r0 - SPANS[step - 1][0], r1 - SPANS[step - 1][0])
            old_head = lambda l: old_head_ref[l, old, :]
            cond_of, store_of, rain = take_framed(3)
        (head_ref,) = take(1)
    v0, v1, v2, v3, inflow_ref, moments_ref = take(6)
    diag_ref, up_ref, dn_ref, ru_ref, rd_ref, xl_ref, xr_ref, flux_ref = take(8)
    if not first:
        res_ref, cap_ref, water_ref, low_cond_ref = take(4)
        head, res, cap, water, low_cond = [
            (lambda l, ref=ref: ref[l]) for ref in (head_ref, res_ref, cap_ref, water_ref, low_cond_ref)
        ]
    basis = (v0, v1, v2, v3)
    section = lax.axis_index("sec")
    band = lax.axis_index("pair") * 2 + lax.axis_index("core")

    if not first:
        change = weights(sums_ref)
        for s in range(SECTIONS):
            total = jnp.zeros((rows, WIDE), F32)
            for q in range(LZ):
                l = s * LZ + q
                h = old_head(l)
                for c, o in zip(change, old_basis):
                    h = h + c * o[l, old_work, :]
                head_ref[l] = h
                saturation, cond, capacity = setup_terms(h, cond_of(l), store_of(l))
                res_ref[l] = recip(cond)
                cap_ref[l] = capacity
                total = total + saturation
            water_ref[s] = total
            low_cond_ref[s] = 0.5 * cond

    flux_ref[0] = rain(step)
    belows = [None] * SECTIONS
    below = None
    for s in reversed(range(SECTIONS)):
        belows[s] = below
        below = water(s) if below is None else below + water(s)
    for s in range(SECTIONS):
        scale = 0.5 if belows[s] is None else 0.5 + 0.5 * belows[s] / (belows[s] + 4.0)
        flux_ref[s + 1] = water(s) * 0.25 * scale * flux_ref[s] + low_cond(s)
        inflow_ref[s] = flux_ref[s, OWN_ROWS - r0 : 2 * OWN_ROWS - r0, 0:OWN_COLS]

    lane = lax.broadcasted_iota(jnp.int32, (span, WIDE), 1)
    col = section * OWN_COLS + lane - jnp.where(lane >= OWN_COLS + HALF, WIDE, 0)
    row = band * OWN_ROWS + (w0 - OWN_ROWS) + lax.broadcasted_iota(jnp.int32, (span, WIDE), 0)
    col_gate = jnp.where((col >= 1) & (col < SECTIONS * OWN_COLS), 2.0, 0.0).astype(F32)
    row_gate = jnp.where((row >= 1) & (row < n_rows_all), 2.0, 0.0).astype(F32)
    kept = slice(own, own + OWN_ROWS)
    none = jnp.zeros((OWN_ROWS, OWN_COLS), F32)

    def faces(l, carry):
        acc, up = carry
        around, tops = res(l), head(l)
        mine, h = around[work], tops[work]
        if l + 1 < NZ:
            dn = 2.0 * recip(mine + res(l + 1)[work])
        else:
            dn = jnp.zeros_like(mine)
        ru = row_gate * recip(mine + turned(around, 1, 0)[work])
        rd = turned(ru, -1, 0)
        xl = col_gate * recip(mine + turned(mine, 1, 1))
        xr = turned(xl, -1, 1)
        diag = cap(l)[work] + up + dn + ru + rd + xl + xr
        inv = recip(diag)
        r = up - dn
        if l % LZ == 0:
            r = r + flux_ref[l // LZ, work, :]
        if l % LZ == LZ - 1:
            r = r - flux_ref[l // LZ + 1, work, :]
        if l > 0:
            r = r + up * (head(l - 1)[work] - h)
        if l + 1 < NZ:
            r = r + dn * (head(l + 1)[work] - h)
        r = r + ru * (turned(tops, 1, 0)[work] - h) + rd * (turned(tops, -1, 0)[work] - h)
        r = r + xl * (turned(h, 1, 1) - h) + xr * (turned(h, -1, 1) - h)
        z = r * inv
        v0[l] = z
        diag_ref[l] = diag[kept, 0:OWN_COLS]
        if l > 0:
            up_ref[l] = up * inv
        if l + 1 < NZ:
            dn_ref[l] = dn * inv
        ru_ref[l] = ru * inv
        rd_ref[l] = rd * inv
        xl_ref[l] = xl * inv
        xr_ref[l] = xr * inv
        return acc + (r * z)[kept, 0:OWN_COLS], dn

    moments = [loop(NZ, faces, (none, jnp.zeros((span, WIDE), F32)))[0]]

    for k in range(1, ITERS):
        src, dst = basis[k - 1], basis[k]

        made = slice(0, SPANS[1][1]) if first and k == ITERS - 1 else slice(0, span)

        def smooth(l, accs):
            v = src[l]
            new = ru_ref[l, made] * turned(v, 1, 0)[made] + rd_ref[l, made] * turned(v, -1, 0)[made]
            near_v = v[made]
            new = new + xl_ref[l, made] * turned(near_v, 1, 1) + xr_ref[l, made] * turned(near_v, -1, 1)
            if l > 0:
                new = new + up_ref[l, made] * src[l - 1, made]
            if l + 1 < NZ:
                new = new + dn_ref[l, made] * src[l + 1, made]
            dst[l, made] = new
            mine = new[kept, 0:OWN_COLS]
            scaled = mine * diag_ref[l]
            return accs[0] + v[kept, 0:OWN_COLS] * scaled, accs[1] + mine * scaled

        moments.extend(loop(NZ, smooth, (none, none)))

    def last(l, acc):
        v = v3[l, own - 8 : own + OWN_ROWS, :]
        mine = v[8:, 0:OWN_COLS]
        pairs = ru_ref[l, kept, 0:OWN_COLS] * turned(v, 1, 0)[8:, 0:OWN_COLS]
        pairs = pairs + xl_ref[l, kept, 0:OWN_COLS] * turned(v, 1, 1)[8:, 0:OWN_COLS]
        if l > 0:
            pairs = pairs + up_ref[l, kept, 0:OWN_COLS] * v3[l - 1, kept, 0:OWN_COLS]
        return acc + 2.0 * mine * diag_ref[l] * pairs

    moments.append(loop(NZ, last, none))

    spot = lax.broadcasted_iota(jnp.int32, (8, 128), 1)
    line = jnp.zeros((8, 128), F32)
    for k, acc in enumerate(moments):
        value = jnp.sum(jnp.sum(acc, axis=0, keepdims=True), axis=1, keepdims=True)
        line = jnp.where(spot == k, value, line)
    moments_ref[...] = line


def last_kernel(sums_ref, head_ref, v0, v1, v2, v3, i0, i1, i2, out_ref):
    change = weights(sums_ref)
    own = OWN_ROWS - WORK[2][0]
    kept = slice(own, own + OWN_ROWS)
    for l in range(NZ):
        h = head_ref[l, OWN_ROWS - SPANS[2][0] : 2 * OWN_ROWS - SPANS[2][0], 0:OWN_COLS]
        for c, o in zip(change, (v0, v1, v2, v3)):
            h = h + c * o[l, kept, 0:OWN_COLS]
        out_ref[l // LZ, l % LZ] = h
    for s in range(SECTIONS):
        for c, i in enumerate((i0, i1, i2)):
            out_ref[s, LZ + c] = i[s]


def shape(*dims):
    return jax.ShapeDtypeStruct(dims, F32)


def near(*dims):
    return pltpu.VMEM(dims, F32)


def held(*arrays, space=pltpu.VMEM):
    return tuple(pltpu.with_memory_space_constraint(x, space) for x in arrays)


def call(kernel, operands, outs, scratch=(), in_specs=None, out_specs=None, **more):
    return pl.pallas_call(
        kernel,
        **more,
        out_shape=outs,
        in_specs=in_specs or [VMEM] * len(operands),
        out_specs=out_specs or jax.tree.map(lambda _: VMEM, outs),
        scratch_shapes=[pltpu.VMEM(dims, F32) if isinstance(dims, tuple) else dims for dims in scratch],
        compiler_params=params(),
    )(*operands)


def join_kernel(parts_ref, head_hbm, flows_hbm, sems):
    copies = []
    for t in range(SECTIONS):
        cols = slice(t * OWN_COLS, (t + 1) * OWN_COLS)
        copies.append(pltpu.make_async_copy(parts_ref.at[t, 0:LZ], head_hbm.at[:, :, cols], sems.at[0, t]))
        copies.append(pltpu.make_async_copy(parts_ref.at[t, LZ : LZ + 3], flows_hbm.at[0, :, :, cols], sems.at[1, t]))
    for copy in copies:
        copy.start()
    for copy in copies:
        copy.wait()


def add_up(moments):
    chips = SECTIONS * lax.axis_size("pair")
    both = moments + lax.ppermute(moments, "core", [(0, 1), (1, 0)])
    rows = lax.all_to_all(jnp.broadcast_to(both[:1, None], (chips, 1, 128)), ("sec", "pair"), 0, 0, tiled=True)
    return rows.reshape(chips, 128)


def body(pressure_start, soil_type, saturated_conductivity, storage_coefficient, rainfall):
    gx = ("pair", "core")
    bands = 2 * lax.axis_size("pair")
    outside = pl.BlockSpec(memory_space=pl.ANY)
    block = (LZ, OWN_ROWS, SECTIONS * OWN_COLS)
    packed = call(
        split_kernel,
        held(pressure_start, soil_type, space=pltpu.HBM),
        near(SECTIONS, 9, OWN_ROWS, OWN_COLS),
        (block, pltpu.VMEM(block, jnp.int32), pltpu.SemaphoreType.DMA((2,))),
        in_specs=[outside] * 2,
    )
    mid = lax.all_to_all(packed, "sec", 0, 0, tiled=True)
    to_beyond, to_chip, rain_own = call(
        edges_kernel,
        held(mid, rainfall),
        [near(REACH * SLOTS + 8, OWN_COLS), near(REACH * SLOTS, OWN_COLS), near(4, OWN_ROWS, OWN_COLS)],
    )
    to_send = call(whole_kernel, held(mid, rain_own), near(SLOTS, OWN_ROWS, OWN_COLS))
    pairs = [(i, i + 1) for i in range(1, bands - 1, 2)]
    beyond = lax.ppermute(to_beyond, gx, pairs + [(j, i) for i, j in pairs])
    chip = lax.ppermute(to_chip, "core", [(0, 1), (1, 0)])
    low, high = call(sides_kernel, held(chip, beyond), [near(SLOTS, OWN_ROWS, OWN_COLS)] * 2)
    tables = jnp.stack([saturated_conductivity, storage_coefficient])
    tables = jnp.broadcast_to(jnp.pad(tables, ((0, 0), (0, 128 - tables.shape[1])))[:, None, :], (2, 8, 128))

    def entered(rows_sent):
        return call(
            enter_kernel,
            (*held(rows_sent), tables),
            [near(n, OWN_ROWS, WIDE) for n in (NZ,) * 5 + (3,) + (SECTIONS,) * 2],
            cost_estimate=pl.CostEstimate(flops=10_000_000, bytes_accessed=4_000_000, transcendentals=300_000),
        )

    parts = [entered(low), entered(to_send), entered(high)]

    def pick(*which):
        return [part[k] for part in parts for k in which]

    inflows = []
    state = None
    for step, (r0, r1) in enumerate(SPANS):
        rows = r1 - r0
        field = (NZ, rows, WIDE)
        basis = (NZ, WORK[step][1] - WORK[step][0], WIDE)
        outs = [near(*field)] + [near(*basis)] * 4
        kernel = functools.partial(step_kernel, step, bands * OWN_ROWS)
        tail = [near(SECTIONS, OWN_ROWS, OWN_COLS), near(8, 128)]
        scratch = [(NZ, OWN_ROWS, OWN_COLS)] + [basis] * 6 + [(SECTIONS + 1, rows, WIDE)]
        if step == 0:
            got = call(kernel, held(*pick(0, 3, 4, 5, 6, 7)), [near(*basis)] * 4 + tail, scratch)
            v = got[:4]
        else:
            state = pick(0, 1, 2, 5) if step == 1 else [head, *pick(1, 2, 5)]
            soil = [field] * 2 + [(SECTIONS, rows, WIDE)] * 2
            got = call(kernel, (sums, *held(*v, *state)), outs + tail, scratch + soil)
            head, v = got[0], got[1:5]
        inflows.append(got[-2])
        sums = add_up(got[-1])
    out = call(last_kernel, (sums, *held(head, *v, *inflows)), near(SECTIONS, 7, OWN_ROWS, OWN_COLS))
    out = lax.all_to_all(out, "sec", 0, 0, tiled=True)
    return call(
        join_kernel,
        held(out),
        [shape(*block), shape(1, 3, *block[1:])],
        (pltpu.SemaphoreType.DMA((2, SECTIONS)),),
        out_specs=[outside] * 2,
    )


def solution(mesh):
    sections, bands = mesh.devices.shape
    gx = ("pair", "core")
    placed = (P("sec", gx, None), P("sec", gx, None), P(), P(), P(None, gx, None))
    return jax.shard_map(
        body,
        mesh=jax.sharding.Mesh(mesh.devices.reshape(sections, bands // 2, 2), ("sec", *gx)),
        in_specs=placed,
        out_specs=(P("sec", gx, None), P("sec", None, gx, None)),
        check_vma=False,
    )
```

```python
import functools

import jax
import jax.numpy as jnp
from jax import lax
from jax.experimental import pallas as pl
from jax.experimental.pallas import tpu as pltpu
from jax.sharding import PartitionSpec as P

ITERS = 4
SECTIONS = 4
LZ = 4
NZ = SECTIONS * LZ
OWN_ROWS = 16
OWN_COLS = 256
WIDE = 384
HALF = 64
EDGE = 16
FRAME = 48
SLOTS = 40
REACH = 13
SPANS = ((0, 48), (0, 40), (8, 40))
WORK = ((0, 48), (8, 40), (8, 40))
F32 = jnp.float32
VMEM = pl.BlockSpec(memory_space=pltpu.VMEM)


def params():
    return pltpu.CompilerParams(vmem_limit_bytes=24 * 1024 * 1024)


def turned(x, by, axis):
    return pltpu.roll(x, by % x.shape[axis], axis)


def lanes(rows):
    return lax.broadcasted_iota(jnp.int32, (rows, 128), 1)


def tail_of(after, before):
    return jnp.where(lanes(after.shape[0]) < EDGE, after, turned(before, 2 * EDGE, 1))


def grouped(tails):
    lane = lanes(tails[0].shape[0])
    tile = tails[0]
    for j in range(1, len(tails)):
        tile = jnp.where(lane >= 2 * EDGE * j, turned(tails[j], 2 * EDGE * j, 1), tile)
    return tile


def spread(tile, count):
    for _ in range(count):
        later = turned(tile, -2 * EDGE, 1)
        yield jnp.where(lanes(tile.shape[0]) < HALF, tile, later)
        tile = later


def split_kernel(head_hbm, soil_hbm, out_ref, head_ref, soil_ref, sems):
    copies = [
        pltpu.make_async_copy(head_hbm, head_ref, sems.at[0]),
        pltpu.make_async_copy(soil_hbm, soil_ref, sems.at[1]),
    ]
    for copy in copies:
        copy.start()
    whole = SECTIONS * OWN_COLS
    for part, ref in enumerate((head_ref, soil_ref)):
        copies[part].wait()
        for target in range(SECTIONS):
            start = target * OWN_COLS
            after, before = (start + OWN_COLS) % whole, (start - 128) % whole
            tails = []
            for q in range(LZ):
                field = ref[q].astype(F32)
                out_ref[target, part * LZ + q] = field[:, start : start + OWN_COLS]
                tails.append(tail_of(field[:, after : after + 128], field[:, before : before + 128]))
            out_ref[target, 2 * LZ, :, 128 * part : 128 * part + 128] = grouped(tails)


def edges_kernel(mid_ref, rain_ref, beyond_ref, chip_ref, rain_out_ref):
    section = lax.axis_index("sec")
    start = pl.multiple_of(section * OWN_COLS, OWN_COLS)
    after = pl.multiple_of(lax.rem(section + 1, SECTIONS) * OWN_COLS, OWN_COLS)
    before = pl.multiple_of(lax.rem(section + SECTIONS - 1, SECTIONS) * OWN_COLS + 128, 128)
    tails = []
    for c in range(3):
        rain_out_ref[c] = rain_ref[c, :, pl.ds(start, OWN_COLS)]
        tails.append(tail_of(rain_ref[c, :, pl.ds(after, 128)], rain_ref[c, :, pl.ds(before, 128)]))
    rain_out_ref[3] = jnp.concatenate([grouped(tails), jnp.zeros((OWN_ROWS, 128), F32)], axis=1)
    first = lax.axis_index("core") == 0
    beyond_ref[REACH * SLOTS :, :] = jnp.zeros((8, OWN_COLS), F32)
    for slot in range(SLOTS):
        field = mid_ref[slot // 9, slot % 9] if slot < 36 else rain_out_ref[slot - 36]
        at = slice(REACH * slot, REACH * slot + REACH)
        top, bottom = field[:REACH], field[OWN_ROWS - REACH :]
        beyond_ref[at, :] = jnp.where(first, top, bottom)
        chip_ref[at, :] = jnp.where(first, bottom, top)


def whole_kernel(mid_ref, rain_ref, out_ref):
    for slot in range(SLOTS):
        out_ref[slot] = mid_ref[slot // 9, slot % 9] if slot < 36 else rain_ref[slot - 36]


def weights(sums_ref):
    total = jnp.sum(sums_ref[...], axis=0, keepdims=True)
    lane = lax.broadcasted_iota(jnp.int32, total.shape, 1)
    m = [jnp.sum(jnp.where(lane == k, total, 0.0), axis=1, keepdims=True) for k in range(8)]
    step_m = [m[k] - m[k + 1] for k in range(7)]
    zero = jnp.zeros_like(m[0])

    def form(poly, other, table):
        result = zero
        for i, a in enumerate(poly):
            for j, b in enumerate(other):
                result = result + a * b * table[i + j]
        return result

    z = [jnp.ones_like(zero)]
    direction = z
    rz = m[0]
    change = [zero] * ITERS
    for turn in range(ITERS):
        below = form(direction, direction, step_m)
        alpha = jnp.where(below > 0.0, rz / jnp.where(below > 0.0, below, 1.0), 0.0)
        for i, a in enumerate(direction):
            change[i] = change[i] + alpha * a
        if turn + 1 < ITERS:
            long = direction + [zero]
            image = [long[i] - (long[i - 1] if i else zero) for i in range(len(long))]
            z = [a - alpha * b for a, b in zip(z + [zero], image)]
            renewed = form(z, z, m)
            beta = jnp.where(rz > 0.0, renewed / jnp.where(rz > 0.0, rz, 1.0), 0.0)
            direction = [a + beta * b for a, b in zip(z, long)]
            rz = renewed
    return change


def loop(n, f, init):
    for i in range(n):
        init = f(i, init)
    return init


def recip(x):
    return pl.reciprocal(x, approx=False)


def setup_terms(h, cond_table, store_table):
    saturation = recip(1.0 + jnp.exp(-h))
    cond = cond_table * (0.05 + saturation * saturation)
    capacity = store_table * (0.1 + saturation * (1.0 - saturation))
    return saturation, cond, capacity


def gather(table, kinds):
    rows, cols = kinds.shape
    parts = []
    for j in range(cols // 128):
        parts.append(
            jnp.concatenate(
                [
                    jnp.take_along_axis(table, kinds[8 * i : 8 * i + 8, 128 * j : 128 * j + 128], axis=1, mode="promise_in_bounds")
                    for i in range(rows // 8)
                ],
                axis=0,
            )
        )
    return jnp.concatenate(parts, axis=1)


def enter_kernel(from_ref, tables_ref, head_ref, cond_ref, store_ref, res_ref, cap_ref, rain_ref, water_ref, low_cond_ref):
    packs = [(rain_ref, 0, 36, 39, 0, 3)]
    for s in range(SECTIONS):
        packs.append((head_ref, s * LZ, 9 * s, 9 * s + 8, 0, LZ))
        packs.append((cond_ref, s * LZ, 9 * s + LZ, 9 * s + 8, 1, LZ))
    for ref, first, slot, halo, tile, count in packs:
        for q, third in enumerate(spread(from_ref[halo, :, 128 * tile : 128 * tile + 128], count)):
            ref[first + q, :, 0:OWN_COLS] = from_ref[slot + q]
            ref[first + q, :, OWN_COLS:WIDE] = third
    for l in range(NZ):
        store_ref[l] = gather(tables_ref[1], cond_ref[l].astype(jnp.int32))
    for l in range(NZ):
        cond_ref[l] = gather(tables_ref[0], cond_ref[l].astype(jnp.int32))
    for s in range(SECTIONS):
        total = jnp.zeros((OWN_ROWS, WIDE), F32)
        for q in range(LZ):
            l = s * LZ + q
            saturation, cond, capacity = setup_terms(head_ref[l], cond_ref[l], store_ref[l])
            res_ref[l] = recip(cond)
            cap_ref[l] = capacity
            total = total + saturation
        water_ref[s] = total
        low_cond_ref[s] = 0.5 * cond


def sides_kernel(chip_ref, beyond_ref, low_ref, high_ref):
    first = lax.axis_index("core") == 0
    for slot in range(SLOTS):
        at = slice(REACH * slot, REACH * slot + REACH)
        chip, beyond = chip_ref[at, :], beyond_ref[at, :]
        gap = jnp.zeros((OWN_ROWS - REACH, OWN_COLS), F32)
        low_ref[slot] = jnp.concatenate([gap, jnp.where(first, beyond, chip)], axis=0)
        high_ref[slot] = jnp.concatenate([jnp.where(first, chip, beyond), gap], axis=0)


def framed(parts, start, stop):
    def read(l):
        pieces = []
        for at, ref in enumerate(parts):
            lo, hi = max(start - 16 * at, 0), min(stop - 16 * at, 16)
            if lo < hi:
                pieces.append(ref[l, lo:hi, :])
        return jnp.concatenate(pieces, axis=0)

    return read


def step_kernel(step, n_rows_all, *refs):
    first = step == 0
    r0, r1 = SPANS[step]
    rows = r1 - r0
    w0, w1 = WORK[step]
    span = w1 - w0
    work = slice(w0 - r0, w1 - r0)
    own = OWN_ROWS - w0
    refs = list(refs)

    def take(n):
        taken, refs[:n] = refs[:n], []
        return taken

    def take_framed(n):
        low, mid, high = take(n), take(n), take(n)
        return [framed(parts, r0, r1) for parts in zip(low, mid, high)]

    if first:
        head, res, cap, rain, water, low_cond = take_framed(6)
    else:
        (sums_ref,) = take(1)
        old_basis = take(ITERS)
        old_work = slice(r0 - WORK[step - 1][0], r1 - WORK[step - 1][0])
        if step == 1:
            old_head, cond_of, store_of, rain = take_framed(4)
        else:
            (old_head_ref,) = take(1)
            old = slice(r0 - SPANS[step - 1][0], r1 - SPANS[step - 1][0])
            old_head = lambda l: old_head_ref[l, old, :]
            cond_of, store_of, rain = take_framed(3)
        (head_ref,) = take(1)
    v0, v1, v2, v3, inflow_ref, moments_ref = take(6)
    diag_ref, up_ref, dn_ref, ru_ref, rd_ref, xl_ref, xr_ref, flux_ref = take(8)
    if not first:
        res_ref, cap_ref, water_ref, low_cond_ref = take(4)
        head, res, cap, water, low_cond = [
            (lambda l, ref=ref: ref[l]) for ref in (head_ref, res_ref, cap_ref, water_ref, low_cond_ref)
        ]
    basis = (v0, v1, v2, v3)
    section = lax.axis_index("sec")
    band = lax.axis_index("pair") * 2 + lax.axis_index("core")

    if not first:
        change = weights(sums_ref)
        for s in range(SECTIONS):
            total = jnp.zeros((rows, WIDE), F32)
            for q in range(LZ):
                l = s * LZ + q
                h = old_head(l)
                for c, o in zip(change, old_basis):
                    h = h + c * o[l, old_work, :]
                head_ref[l] = h
                saturation, cond, capacity = setup_terms(h, cond_of(l), store_of(l))
                res_ref[l] = recip(cond)
                cap_ref[l] = capacity
                total = total + saturation
            water_ref[s] = total
            low_cond_ref[s] = 0.5 * cond

    flux_ref[0] = rain(step)
    belows = [None] * SECTIONS
    below = None
    for s in reversed(range(SECTIONS)):
        belows[s] = below
        below = water(s) if below is None else below + water(s)
    for s in range(SECTIONS):
        scale = 0.5 if belows[s] is None else 0.5 + 0.5 * belows[s] / (belows[s] + 4.0)
        flux_ref[s + 1] = water(s) * 0.25 * scale * flux_ref[s] + low_cond(s)
        inflow_ref[s] = flux_ref[s, OWN_ROWS - r0 : 2 * OWN_ROWS - r0, 0:OWN_COLS]

    lane = lax.broadcasted_iota(jnp.int32, (span, WIDE), 1)
    col = section * OWN_COLS + lane - jnp.where(lane >= OWN_COLS + HALF, WIDE, 0)
    row = band * OWN_ROWS + (w0 - OWN_ROWS) + lax.broadcasted_iota(jnp.int32, (span, WIDE), 0)
    col_gate = jnp.where((col >= 1) & (col < SECTIONS * OWN_COLS), 2.0, 0.0).astype(F32)
    row_gate = jnp.where((row >= 1) & (row < n_rows_all), 2.0, 0.0).astype(F32)
    kept = slice(own, own + OWN_ROWS)
    none = jnp.zeros((OWN_ROWS, OWN_COLS), F32)

    def faces(l, carry):
        acc, up = carry
        around, tops = res(l), head(l)
        mine, h = around[work], tops[work]
        if l + 1 < NZ:
            dn = 2.0 * recip(mine + res(l + 1)[work])
        else:
            dn = jnp.zeros_like(mine)
        ru = row_gate * recip(mine + turned(around, 1, 0)[work])
        rd = turned(ru, -1, 0)
        xl = col_gate * recip(mine + turned(mine, 1, 1))
        xr = turned(xl, -1, 1)
        diag = cap(l)[work] + up + dn + ru + rd + xl + xr
        inv = recip(diag)
        r = up - dn
        if l % LZ == 0:
            r = r + flux_ref[l // LZ, work, :]
        if l % LZ == LZ - 1:
            r = r - flux_ref[l // LZ + 1, work, :]
        if l > 0:
            r = r + up * (head(l - 1)[work] - h)
        if l + 1 < NZ:
            r = r + dn * (head(l + 1)[work] - h)
        r = r + ru * (turned(tops, 1, 0)[work] - h) + rd * (turned(tops, -1, 0)[work] - h)
        r = r + xl * (turned(h, 1, 1) - h) + xr * (turned(h, -1, 1) - h)
        z = r * inv
        v0[l] = z
        diag_ref[l] = diag[kept, 0:OWN_COLS]
        if l > 0:
            up_ref[l] = up * inv
        if l + 1 < NZ:
            dn_ref[l] = dn * inv
        ru_ref[l] = ru * inv
        rd_ref[l] = rd * inv
        xl_ref[l] = xl * inv
        xr_ref[l] = xr * inv
        return acc + (r * z)[kept, 0:OWN_COLS], dn

    moments = [loop(NZ, faces, (none, jnp.zeros((span, WIDE), F32)))[0]]

    for k in range(1, ITERS):
        src, dst = basis[k - 1], basis[k]

        made = slice(0, SPANS[1][1]) if first and k == ITERS - 1 else slice(0, span)

        def smooth(l, accs):
            v = src[l]
            new = ru_ref[l, made] * turned(v, 1, 0)[made] + rd_ref[l, made] * turned(v, -1, 0)[made]
            near_v = v[made]
            new = new + xl_ref[l, made] * turned(near_v, 1, 1) + xr_ref[l, made] * turned(near_v, -1, 1)
            if l > 0:
                new = new + up_ref[l, made] * src[l - 1, made]
            if l + 1 < NZ:
                new = new + dn_ref[l, made] * src[l + 1, made]
            dst[l, made] = new
            mine = new[kept, 0:OWN_COLS]
            scaled = mine * diag_ref[l]
            return accs[0] + v[kept, 0:OWN_COLS] * scaled, accs[1] + mine * scaled

        moments.extend(loop(NZ, smooth, (none, none)))

    def last(l, acc):
        v = v3[l, own - 8 : own + OWN_ROWS, :]
        mine = v[8:, 0:OWN_COLS]
        pairs = ru_ref[l, kept, 0:OWN_COLS] * turned(v, 1, 0)[8:, 0:OWN_COLS]
        pairs = pairs + xl_ref[l, kept, 0:OWN_COLS] * turned(v, 1, 1)[8:, 0:OWN_COLS]
        if l > 0:
            pairs = pairs + up_ref[l, kept, 0:OWN_COLS] * v3[l - 1, kept, 0:OWN_COLS]
        return acc + 2.0 * mine * diag_ref[l] * pairs

    moments.append(loop(NZ, last, none))

    spot = lax.broadcasted_iota(jnp.int32, (8, 128), 1)
    line = jnp.zeros((8, 128), F32)
    for k, acc in enumerate(moments):
        value = jnp.sum(jnp.sum(acc, axis=0, keepdims=True), axis=1, keepdims=True)
        line = jnp.where(spot == k, value, line)
    moments_ref[...] = line


def last_kernel(sums_ref, head_ref, v0, v1, v2, v3, i0, i1, i2, *out_refs):
    change = weights(sums_ref)
    own = OWN_ROWS - WORK[2][0]
    kept = slice(own, own + OWN_ROWS)
    section = lax.axis_index("sec")
    for on, out_ref in enumerate(out_refs):
        target = lax.rem(section + on, SECTIONS)
        for q in range(LZ):
            l = target * LZ + q
            h = head_ref[l, OWN_ROWS - SPANS[2][0] : 2 * OWN_ROWS - SPANS[2][0], 0:OWN_COLS]
            for c, o in zip(change, (v0, v1, v2, v3)):
                h = h + c * o[l, kept, 0:OWN_COLS]
            out_ref[q] = h
        for c, i in enumerate((i0, i1, i2)):
            out_ref[LZ + c] = i[target]


def shape(*dims):
    return jax.ShapeDtypeStruct(dims, F32)


def near(*dims):
    return pltpu.VMEM(dims, F32)


def held(*arrays, space=pltpu.VMEM):
    return tuple(pltpu.with_memory_space_constraint(x, space) for x in arrays)


def call(kernel, operands, outs, scratch=(), in_specs=None, out_specs=None, **more):
    return pl.pallas_call(
        kernel,
        **more,
        out_shape=outs,
        in_specs=in_specs or [VMEM] * len(operands),
        out_specs=out_specs or jax.tree.map(lambda _: VMEM, outs),
        scratch_shapes=[pltpu.VMEM(dims, F32) if isinstance(dims, tuple) else dims for dims in scratch],
        compiler_params=params(),
    )(*operands)


def join_kernel(p0, p1, p2, p3, head_hbm, flows_hbm, sems):
    section = lax.axis_index("sec")
    copies = []
    for on, part in enumerate((p0, p1, p2, p3)):
        source = lax.rem(section + SECTIONS - on, SECTIONS)
        cols = pl.ds(pl.multiple_of(source * OWN_COLS, OWN_COLS), OWN_COLS)
        copies.append(pltpu.make_async_copy(part.at[0:LZ], head_hbm.at[:, :, cols], sems.at[0, on]))
        copies.append(pltpu.make_async_copy(part.at[LZ : LZ + 3], flows_hbm.at[0, :, :, cols], sems.at[1, on]))
    for copy in copies:
        copy.start()
    for copy in copies:
        copy.wait()


def add_up(moments):
    chips = SECTIONS * lax.axis_size("pair")
    both = moments + lax.ppermute(moments, "core", [(0, 1), (1, 0)])
    rows = lax.all_to_all(jnp.broadcast_to(both[:1, None], (chips, 1, 128)), ("sec", "pair"), 0, 0, tiled=True)
    return rows.reshape(chips, 128)


def body(pressure_start, soil_type, saturated_conductivity, storage_coefficient, rainfall):
    gx = ("pair", "core")
    bands = 2 * lax.axis_size("pair")
    outside = pl.BlockSpec(memory_space=pl.ANY)
    block = (LZ, OWN_ROWS, SECTIONS * OWN_COLS)
    packed = call(
        split_kernel,
        held(pressure_start, soil_type, space=pltpu.HBM),
        near(SECTIONS, 9, OWN_ROWS, OWN_COLS),
        (block, pltpu.VMEM(block, jnp.int32), pltpu.SemaphoreType.DMA((2,))),
        in_specs=[outside] * 2,
    )
    mid = lax.all_to_all(packed, "sec", 0, 0, tiled=True)
    to_beyond, to_chip, rain_own = call(
        edges_kernel,
        held(mid, rainfall),
        [near(REACH * SLOTS + 8, OWN_COLS), near(REACH * SLOTS, OWN_COLS), near(4, OWN_ROWS, OWN_COLS)],
    )
    to_send = call(whole_kernel, held(mid, rain_own), near(SLOTS, OWN_ROWS, OWN_COLS))
    pairs = [(i, i + 1) for i in range(1, bands - 1, 2)]
    beyond = lax.ppermute(to_beyond, gx, pairs + [(j, i) for i, j in pairs])
    chip = lax.ppermute(to_chip, "core", [(0, 1), (1, 0)])
    low, high = call(sides_kernel, held(chip, beyond), [near(SLOTS, OWN_ROWS, OWN_COLS)] * 2)
    tables = jnp.stack([saturated_conductivity, storage_coefficient])
    tables = jnp.broadcast_to(jnp.pad(tables, ((0, 0), (0, 128 - tables.shape[1])))[:, None, :], (2, 8, 128))

    def entered(rows_sent):
        return call(
            enter_kernel,
            (*held(rows_sent), tables),
            [near(n, OWN_ROWS, WIDE) for n in (NZ,) * 5 + (3,) + (SECTIONS,) * 2],
            cost_estimate=pl.CostEstimate(flops=10_000_000, bytes_accessed=4_000_000, transcendentals=300_000),
        )

    parts = [entered(low), entered(to_send), entered(high)]

    def pick(*which):
        return [part[k] for part in parts for k in which]

    inflows = []
    state = None
    for step, (r0, r1) in enumerate(SPANS):
        rows = r1 - r0
        field = (NZ, rows, WIDE)
        basis = (NZ, WORK[step][1] - WORK[step][0], WIDE)
        outs = [near(*field)] + [near(*basis)] * 4
        kernel = functools.partial(step_kernel, step, bands * OWN_ROWS)
        tail = [near(SECTIONS, OWN_ROWS, OWN_COLS), near(8, 128)]
        scratch = [(NZ, OWN_ROWS, OWN_COLS)] + [basis] * 6 + [(SECTIONS + 1, rows, WIDE)]
        if step == 0:
            got = call(kernel, held(*pick(0, 3, 4, 5, 6, 7)), [near(*basis)] * 4 + tail, scratch)
            v = got[:4]
        else:
            state = pick(0, 1, 2, 5) if step == 1 else [head, *pick(1, 2, 5)]
            soil = [field] * 2 + [(SECTIONS, rows, WIDE)] * 2
            got = call(kernel, (sums, *held(*v, *state)), outs + tail, scratch + soil)
            head, v = got[0], got[1:5]
        inflows.append(got[-2])
        sums = add_up(got[-1])
    out = call(last_kernel, (sums, *held(head, *v, *inflows)), [near(7, OWN_ROWS, OWN_COLS)] * SECTIONS)
    out = list(out)
    for on in (2, 1, 3):
        out[on] = lax.ppermute(out[on], "sec", [(i, (i + on) % SECTIONS) for i in range(SECTIONS)])
    return call(
        join_kernel,
        held(*out),
        [shape(*block), shape(1, 3, *block[1:])],
        (pltpu.SemaphoreType.DMA((2, SECTIONS)),),
        out_specs=[outside] * 2,
    )


def solution(mesh):
    sections, bands = mesh.devices.shape
    gx = ("pair", "core")
    placed = (P("sec", gx, None), P("sec", gx, None), P(), P(), P(None, gx, None))
    return jax.shard_map(
        body,
        mesh=jax.sharding.Mesh(mesh.devices.reshape(sections, bands // 2, 2), ("sec", *gx)),
        in_specs=placed,
        out_specs=(P("sec", gx, None), P("sec", None, gx, None)),
        check_vma=False,
    )
```
